128 devices in a mesh: replica: 16 (over x, y), tensor: 8 (over z, core).
Axes of the slice: x: 4, y: 4, z: 4, core: 2. Of those that a mesh axis runs over, the one named last changes fastest.
Arguments:
- hidden: bfloat16 [2048, 8192], P('replica', 'tensor'), may hold values from -6 to 6
- query_weight: bfloat16 [8192, 4096], P(None, 'tensor'), may hold values from -0.0625 to 0.0625
- keyvalue_weight: bfloat16 [2, 8192, 1024], P(None, None, 'tensor'), may hold values from -0.0625 to 0.0625
- output_weight: bfloat16 [4096, 8192], P('tensor'), may hold values from -0.09375 to 0.09375
- adapter_down_maps: bfloat16 [128, 8192, 48], P('replica', 'tensor'), may hold values from -0.0625 to 0.0625
- adapter_up_query: bfloat16 [128, 16, 4096], P('replica', None, 'tensor'), may hold values from -0.375 to 0.375
- adapter_up_keyvalue: bfloat16 [128, 2, 16, 1024], P('replica', None, None, 'tensor'), may hold values from -0.375 to 0.375
- adapter_down_output: bfloat16 [128, 4096, 16], P('replica', 'tensor'), may hold values from -0.09375 to 0.09375
- adapter_up_output: bfloat16 [128, 16, 8192], P('replica', None, 'tensor'), may hold values from -0.375 to 0.375
- cached_keys: bfloat16 [2048, 8, 128, 128], P('replica', 'tensor'), may hold values from -420 to 420
- cached_values: bfloat16 [2048, 8, 128, 128], P('replica', 'tensor'), may hold values from -18 to 18
- context_lengths: int32 [2048], P('replica'), may hold values from 2 to 128, as said below
- request_list_slots: int32 [2048], P('replica'), may hold values from 0 to 31
- group_adapter_lists: int32 [16, 32], replicated, may hold values from 0 to 127, as said below
Outputs:
- mixed_out: bfloat16 [2048, 8192], P('replica', 'tensor')
The draws below stay inside these ranges and needn't reach their ends.
Inputs may be any that keep to these rules, and one draw needn't show every extreme that they name: `context_lengths`: in every group of 128 consecutive requests one has exactly 128. `group_adapter_lists`: each row names 32 different adapters; at most 4 of a row lie in one block of 8 consecutive adapter numbers, and in every row some block holds exactly 4.
All inputs are finite; a program needn't handle non-finite values.
Results may differ from the reference program's by a relative error of at most 0.012.
The reference program's roundings to bfloat16 on the way count: a program that leaves them out, or rounds other values in their place, can miss the bound.
Values may be sent and summed in bfloat16 or wider, within the bound.
A program may use at most 128 MiB of HBM per device.

```python
import math
import jax
import jax.numpy as jnp
import numpy as np
from jax import lax

MODEL_WIDTH = 8192
KV_HEADS = 8
HEAD = 128
HEADS_Q = 32
ADAPTER_RANK = 16
LIST = 32
ADAPT_DEV = 8
CTX = 128
REQ = 128
QUERY_FEATURES = 4096
KEY_FEATURES = 1024
ADAPTER_COUNT = 128
REQUESTS = 2048
CAP = 4


def draw_cached_keys(key, part):
    key = jax.random.fold_in(key, 11)
    array_shape = (REQUESTS, KV_HEADS, CTX, HEAD)
    entries = jax.random.truncated_normal(key, -6.0, 6.0, array_shape, jnp.float32)
    return entries.astype(jnp.bfloat16)


def draw_context_lengths(key, part):
    key = jax.random.fold_in(key, 12)
    groups = REQUESTS // REQ
    first_key = jax.random.fold_in(key, 1)
    second_key = jax.random.fold_in(key, 2)
    lengths = jax.random.randint(first_key, (groups, REQ), 2, CTX + 1)
    chosen = jax.random.randint(second_key, (groups,), 0, REQ)
    marked = jnp.arange(REQ)[None, :] == chosen[:, None]
    return jnp.where(marked, CTX, lengths).reshape(-1).astype(jnp.int32)


def draw_group_adapter_lists(key, part):
    key = jax.random.fold_in(key, 13)
    owners = ADAPTER_COUNT // ADAPT_DEV
    groups = REQUESTS // REQ
    base_count = LIST // owners
    moves = 4 * owners

    def one_group(group_key):
        target_key = jax.random.fold_in(group_key, 1)
        source_key = jax.random.fold_in(group_key, 2)
        receive_key = jax.random.fold_in(group_key, 3)
        local_key = jax.random.fold_in(group_key, 4)
        order_key = jax.random.fold_in(group_key, 5)
        target = jax.random.randint(target_key, (), 0, owners)
        counts = jnp.full((owners,), base_count, jnp.int32)
        counts = counts.at[target].set(CAP)
        donors = (target + 1 + jnp.arange(CAP - base_count)) % owners
        counts = counts.at[donors].add(-1)
        sources = jax.random.randint(source_key, (moves,), 0, owners)
        receivers = jax.random.randint(receive_key, (moves,), 0, owners)

        def transfer(index, tallies):
            source = sources[index]
            target_id = receivers[index]
            allowed = (tallies[source] > 0) & (tallies[target_id] < CAP) & (source != target_id)
            moved = allowed.astype(jnp.int32)
            return tallies.at[source].add(-moved).at[target_id].add(moved)
        counts = lax.fori_loop(0, moves, transfer, counts)
        local_order = jax.vmap(lambda member: jax.random.permutation(member, ADAPT_DEV))(jax.random.split(local_key, owners))
        adapter_ids = jnp.arange(owners)[:, None] * ADAPT_DEV + local_order
        valid = jnp.arange(ADAPT_DEV)[None, :] < counts[:, None]
        order_score = jax.random.permutation(order_key, owners * ADAPT_DEV)
        sort_keys = jnp.where(valid.reshape(-1), order_score, order_score + owners * ADAPT_DEV)
        picked = jnp.argsort(sort_keys, stable=True)[:LIST]
        return jnp.take(adapter_ids.reshape(-1), picked, axis=0)
    return jax.vmap(one_group)(jax.random.split(key, groups)).astype(jnp.int32)


def place_ends(values, stream_key, smallest, high):
    dims = values.shape
    spot = [jax.random.randint(jax.random.fold_in(stream_key, axis), (), 0, dims[axis]) for axis in range(len(dims))]
    values = values.at[tuple(spot)].set(smallest)
    longest = dims.index(max(dims))
    spot[longest] = (spot[longest] + 1) % dims[longest]
    return values.at[tuple(spot)].set(high)


def steps_of(rng, dims, pieces, smallest, top_value):
    gain = 1.0
    for axis_at, parts in pieces:
        draws = jax.random.uniform(jax.random.fold_in(jax.random.fold_in(rng, 6), axis_at), (parts,), jnp.float32, smallest / len(pieces), top_value / len(pieces))
        gain = gain * jnp.repeat(jnp.exp(draws), dims[axis_at] // parts).reshape((-1,) + (1,) * (len(dims) - 1 - axis_at))
    return gain


def rank_table(amount, slope):
    loads = [(1 << 20) // math.isqrt(grade ** slope) + 1 for grade in range(1, amount + 1)]
    scale = 1 + sum(loads) // (1 << 30)
    return np.cumsum(np.array([max(1, weight // scale) for weight in loads]))


def skewed_ids(own_key, shape, number_of, slope):
    listing = rank_table(number_of, slope)
    pick = jax.random.randint(jax.random.fold_in(own_key, 1), shape, 0, int(listing[number_of - 1]))
    rank = jnp.searchsorted(jnp.asarray(listing, jnp.int32), pick, side="right")
    return jax.random.permutation(jax.random.fold_in(own_key, 2), number_of)[rank].astype(jnp.int32)


def scatter_about(rng, shape, scale, bound, cuts=(), held_as=jnp.bfloat16):
    level = steps_of(rng, shape, cuts, -0.22, 0.18) if cuts else 1.0
    drawn = jax.random.normal(rng, shape, jnp.float32) * scale * level
    return jnp.minimum(jnp.maximum(drawn, -bound), bound).astype(held_as)


def setup_inputs(seed: int = 0) -> dict:
    seeds = jax.random.split(jax.random.key(seed), 15)
    hidden = scatter_about(seeds[0], (REQUESTS, MODEL_WIDTH), 1.0, 6.0, ((0, 16), (1, 8)))
    query_weight = scatter_about(seeds[1], (MODEL_WIDTH, QUERY_FEATURES), MODEL_WIDTH ** -0.5, 0.0625, ((1, 8),))
    keyvalue_weight = scatter_about(seeds[2], (2, MODEL_WIDTH, KEY_FEATURES), MODEL_WIDTH ** -0.5, 0.0625, ((2, 8),))
    output_weight = scatter_about(seeds[3], (QUERY_FEATURES, MODEL_WIDTH), QUERY_FEATURES ** -0.5, 0.09375, ((0, 8),))
    adapter_down_maps = scatter_about(seeds[4], (ADAPTER_COUNT, MODEL_WIDTH, 3 * ADAPTER_RANK), MODEL_WIDTH ** -0.5, 0.0625, ((0, 16), (1, 8)))
    adapter_up_query = scatter_about(seeds[5], (ADAPTER_COUNT, ADAPTER_RANK, QUERY_FEATURES), (16 * ADAPTER_RANK) ** -0.5, 0.375, ((0, 16), (2, 8)))
    adapter_up_keyvalue = scatter_about(seeds[6], (ADAPTER_COUNT, 2, ADAPTER_RANK, KEY_FEATURES), (16 * ADAPTER_RANK) ** -0.5, 0.375, ((0, 16), (3, 8)))
    adapter_down_output = scatter_about(seeds[7], (ADAPTER_COUNT, QUERY_FEATURES, ADAPTER_RANK), QUERY_FEATURES ** -0.5, 0.09375, ((0, 16), (1, 8)))
    adapter_up_output = scatter_about(seeds[8], (ADAPTER_COUNT, ADAPTER_RANK, MODEL_WIDTH), (16 * ADAPTER_RANK) ** -0.5, 0.375, ((0, 16), (2, 8)))
    cached_keys = draw_cached_keys(jax.random.fold_in(seeds[14], 71), 0)
    cached_values = scatter_about(seeds[10], (REQUESTS, KV_HEADS, CTX, HEAD), 3.0, 18.0, ((0, 16), (1, 8)))
    context_lengths = draw_context_lengths(jax.random.fold_in(seeds[14], 71), 0)
    request_list_slots = place_ends(skewed_ids(seeds[12], (REQUESTS,), LIST, 2), jax.random.fold_in(seeds[12], 3), 0, LIST - 1).astype(jnp.int32)
    group_adapter_lists = draw_group_adapter_lists(jax.random.fold_in(seeds[14], 71), 0)
    return dict(hidden=hidden, query_weight=query_weight, keyvalue_weight=keyvalue_weight, output_weight=output_weight, adapter_down_maps=adapter_down_maps, adapter_up_query=adapter_up_query, adapter_up_keyvalue=adapter_up_keyvalue, adapter_down_output=adapter_down_output, adapter_up_output=adapter_up_output, cached_keys=cached_keys, cached_values=cached_values, context_lengths=context_lengths, request_list_slots=request_list_slots, group_adapter_lists=group_adapter_lists)


ADAPTER_SCALE = 2.0
ROPE_BASE = 500000.0

def rotate(values, positions):
    half_size = values.shape[-1] // 2
    frequency = ROPE_BASE ** (-(jnp.arange(half_size, dtype=jnp.float32) * 2.0) / values.shape[-1])
    angles = positions.astype(jnp.float32)[:, None, None] * frequency[None, None, :]
    cosine_terms = jnp.cos(angles)
    sine_terms = jnp.sin(angles)
    front = values[..., :half_size]
    back = values[..., half_size:]
    return jnp.concatenate([front * cosine_terms - back * sine_terms, back * cosine_terms + front * sine_terms], axis=-1)

def attend(queries, new_key, new_value, cached_keys, cached_values, context_lengths):
    score_scale = 1.0 / jnp.sqrt(jnp.float32(queries.shape[-1]))
    precise_mode = lax.Precision.HIGHEST
    scores = jnp.einsum('rkgh,rkch->rkgc', queries.astype(jnp.float32), cached_keys.astype(jnp.float32), precision=precise_mode) * score_scale
    self_score = jnp.einsum('rkgh,rkh->rkg', queries.astype(jnp.float32), new_key.astype(jnp.float32), precision=precise_mode) * score_scale
    valid = (jnp.arange(cached_keys.shape[2], dtype=jnp.int32)[None, :] < context_lengths[:, None])[:, None, None, :]
    highest = jnp.maximum(lax.optimization_barrier(jnp.max(jnp.where(valid, scores, -1e+30), axis=-1)), self_score)
    weights = jnp.where(valid, jnp.exp(scores - highest[..., None]), 0.0)
    self_weight = jnp.exp(self_score - highest)
    total = lax.optimization_barrier(jnp.sum(weights, axis=-1)) + self_weight
    rounded = (weights / total[..., None]).astype(jnp.bfloat16)
    self_rounded = (self_weight / total).astype(jnp.bfloat16)
    mixed = jnp.einsum('rkgc,rkch->rkgh', rounded.astype(jnp.float32), cached_values.astype(jnp.float32), precision=precise_mode)
    mixed = mixed + self_rounded.astype(jnp.float32)[..., None] * new_value.astype(jnp.float32)[:, :, None, :]
    return mixed.astype(jnp.bfloat16).reshape(queries.shape[0], -1)

def reference(hidden, query_weight, keyvalue_weight, output_weight, adapter_down_maps, adapter_up_query, adapter_up_keyvalue, adapter_down_output, adapter_up_output, cached_keys, cached_values, context_lengths, request_list_slots, group_adapter_lists):
    groups = group_adapter_lists.shape[0]
    precise_mode = lax.Precision.HIGHEST

    def by_group(array):
        return array.reshape((groups, -1) + array.shape[1:])

    def one_group(items):
        input_rows, keys_here, values_here, lengths, slot_ids, wanted = items
        request_rows = input_rows.shape[0]
        adapter_choice = jnp.take(wanted, slot_ids, axis=0)
        frozen_query = jnp.dot(input_rows, query_weight, preferred_element_type=jnp.float32)
        frozen_key = jnp.dot(input_rows, keyvalue_weight[0], preferred_element_type=jnp.float32)
        frozen_value = jnp.dot(input_rows, keyvalue_weight[1], preferred_element_type=jnp.float32)
        adapter_rows = jnp.take(adapter_down_maps, adapter_choice, axis=0).astype(jnp.float32)
        reduced_rows = jnp.einsum('hj,hju->hu', input_rows.astype(jnp.float32), adapter_rows, precision=precise_mode).astype(jnp.bfloat16)
        raised_query = jnp.einsum('vj,vjw->vw', reduced_rows[:, :ADAPTER_RANK].astype(jnp.float32), jnp.take(adapter_up_query, adapter_choice, axis=0).astype(jnp.float32), precision=precise_mode)
        raised_keyvalue = jnp.einsum('nxi,nxit->xnt', reduced_rows[:, ADAPTER_RANK:].reshape(request_rows, 2, ADAPTER_RANK).astype(jnp.float32), jnp.take(adapter_up_keyvalue, adapter_choice, axis=0).astype(jnp.float32), precision=precise_mode)
        unrotated_query = frozen_query + ADAPTER_SCALE * raised_query
        unrotated_key = frozen_key + ADAPTER_SCALE * raised_keyvalue[0]
        unrotated_value = frozen_value + ADAPTER_SCALE * raised_keyvalue[1]
        queries = rotate(unrotated_query.reshape(request_rows, HEADS_Q, HEAD), lengths).astype(jnp.bfloat16)
        queries = queries.reshape(request_rows, KV_HEADS, HEADS_Q // KV_HEADS, HEAD)
        new_key = rotate(unrotated_key.reshape(request_rows, KV_HEADS, HEAD), lengths).astype(jnp.bfloat16)
        new_value = unrotated_value.reshape(request_rows, KV_HEADS, HEAD).astype(jnp.bfloat16)
        attention_output = attend(queries, new_key, new_value, keys_here, values_here, lengths)
        projected_rows = jnp.dot(attention_output, output_weight, preferred_element_type=jnp.float32)
        reduced_output = jnp.einsum('xz,xzn->xn', attention_output.astype(jnp.float32), jnp.take(adapter_down_output, adapter_choice, axis=0).astype(jnp.float32), precision=precise_mode).astype(jnp.bfloat16)
        raised_output = jnp.einsum('jt,jtc->jc', reduced_output.astype(jnp.float32), jnp.take(adapter_up_output, adapter_choice, axis=0).astype(jnp.float32), precision=precise_mode)
        return (projected_rows + ADAPTER_SCALE * raised_output).astype(jnp.bfloat16)
    result = lax.map(one_group, (by_group(hidden), by_group(cached_keys), by_group(cached_values), by_group(context_lengths), by_group(request_list_slots), group_adapter_lists))
    return result.reshape(-1, hidden.shape[1])
```

```python
import functools

import jax
import jax.numpy as jnp
from jax import lax
from jax.experimental import pallas as pl
from jax.experimental.pallas import tpu as pltpu
from jax.sharding import PartitionSpec as P

ADAPTER_SCALE = 2.0
ROPE_BASE = 500000.0
MESH = pl.DeviceIdType.MESH
BF16 = jnp.bfloat16
F32 = jnp.float32
NT = (((1,), (1,)), ((), ()))
NEGATIVE = -1e30
SENDS = 104
LOCALS = 56


def mm(a, b):
    return jnp.dot(a, b, preferred_element_type=F32)


def kernel(
    hidden, ids_rows, ids_col, cosines, sines, lengths,
    query_w, kv_w, out_w, down, up_q, up_kv, down_o, up_o, keys, values,
    out,
    z_all, h_a, h_b, d_a, d_b, u_all, p_all, o_all, w_all, w_out, k_all, v_all,
    acc, low_send_a, low_recv_a, low_send_b, low_recv_b, low_parts, out_parts,
    q_rows, key_rows, value_rows, length_rows, mixed_rows,
    sib_send, sib_recv, far_send, far_plus, far_minus, near_send, near_recv, own_sum,
    send_sem, recv_sem, local_sem,
):
    replica = lax.axis_index("replica")
    t = lax.axis_index("tensor")
    x, y = replica // 4, replica % 4
    z, c = t // 2, t % 2
    other = 1 - c

    def wrap(v):
        return lax.rem(v + 4, 4)

    def at_x(d):
        return (wrap(x + d) * 4 + y, t)

    def at_y(d):
        return (x * 4 + wrap(y + d), t)

    def at_z(d):
        return (replica, wrap(z + d) * 2 + c)

    sibling = (replica, z * 2 + other)

    counts = {"send": 0, "local": 0}
    sent = []

    def send(src, dst, device):
        i = counts["send"]
        counts["send"] = i + 1
        copy = pltpu.make_async_remote_copy(
            src_ref=src, dst_ref=dst, send_sem=send_sem.at[i], recv_sem=recv_sem.at[i],
            device_id=device, device_id_type=MESH,
        )
        copy.start()
        sent.append(copy)
        return copy

    def local(src, dst):
        i = counts["local"]
        counts["local"] = i + 1
        copy = pltpu.make_async_copy(src, dst, local_sem.at[i])
        copy.start()
        return copy

    barrier = pltpu.get_barrier_semaphore()
    partners = [at_x(d) for d in (1, 2, 3)] + [at_y(d) for d in (1, 2, 3)]
    partners += [(replica, lax.rem(t + d, 8)) for d in range(1, 8)]
    for partner in partners:
        pl.semaphore_signal(barrier, inc=1, device_id=partner, device_id_type=MESH)

    own_h = [
        local(hidden, z_all.at[t]),
        local(hidden.at[:, 0:512], h_a.at[x, 0:128]),
        local(ids_rows, h_a.at[x, 128:144]),
        local(hidden.at[:, 512:1024], h_b.at[y, 0:128]),
        local(ids_rows, h_b.at[y, 128:144]),
    ]
    own_d = [
        local(down.at[:, :, 0:512], d_a.at[y]),
        local(down.at[:, :, 512:1024], d_b.at[x]),
    ]
    own_u = [
        local(up_q, u_all.at[x, y, :, :, 0:512]),
        local(up_kv.at[:, 0], u_all.at[x, y, :, :, 512:640]),
        local(up_kv.at[:, 1], u_all.at[x, y, :, :, 640:768]),
    ]
    own_o = [
        local(down_o, p_all.at[x, y]),
        local(up_o, o_all.at[x, y]),
    ]
    pl.semaphore_wait(barrier, len(partners))

    def ring_one(part, own, device):
        return (
            send(part(own), part(own), device(1)),
            send(part(own), part(own), device(-1)),
        )

    def ring_two(first, part_lo, part_hi, own, device):
        first[0].wait_recv()
        first[1].wait_recv()
        before, after = wrap(own - 1), wrap(own + 1)
        return (
            send(part_lo(before), part_lo(before), device(1)),
            send(part_hi(after), part_hi(after), device(-1)),
        )

    def gather_one(pool):
        return (
            ring_one(lambda i: pool.at[i, y, 0:4], x, at_x),
            ring_one(lambda i: pool.at[x, i, 4:8], y, at_y),
        )

    def gather_two(pool, a, b):
        return (
            ring_two(a, lambda i: pool.at[i, y, 0:2], lambda i: pool.at[i, y, 2:4], x, at_x),
            ring_two(b, lambda i: pool.at[x, i, 4:6], lambda i: pool.at[x, i, 6:8], y, at_y),
        )

    def gather_three(pool):
        return (
            ring_one(lambda i: pool.at[:, i, 0:4], y, at_y),
            ring_one(lambda i: pool.at[i, :, 4:8], x, at_x),
        )

    def gather_four(pool, a, b):
        return (
            ring_two(a, lambda i: pool.at[:, i, 0:2], lambda i: pool.at[:, i, 2:4], y, at_y),
            ring_two(b, lambda i: pool.at[i, :, 4:6], lambda i: pool.at[i, :, 6:8], x, at_x),
        )

    def landed(copies):
        for copy in copies:
            copy.wait_recv()

    for copy in own_h:
        copy.wait()
    ha1 = ring_one(lambda i: h_a.at[i], x, at_x)
    hb1 = ring_one(lambda i: h_b.at[i], y, at_y)
    z1 = ring_one(lambda i: z_all.at[i * 2 + c], z, at_z)
    s0 = send(z_all.at[t], z_all.at[t], sibling)
    for copy in own_d:
        copy.wait()
    da1 = ring_one(lambda i: d_a.at[i], y, at_y)
    db1 = ring_one(lambda i: d_b.at[i], x, at_x)

    w_copies = []
    for d in range(8):
        i = lax.rem(t + d, 8)
        w_copies.append(local(query_w.at[i], w_all.at[i, :, 0:512]))
        w_copies.append(local(kv_w.at[0, i], w_all.at[i, :, 512:640]))
        w_copies.append(local(kv_w.at[1, i], w_all.at[i, :, 640:768]))
    k_copy = local(keys, k_all)
    v_copy = local(values, v_all)
    o_copies = []
    for d in (2, 1, 3, 0):
        for core in (other, c):
            i = wrap(z + d) * 2 + core
            columns = pl.ds(pl.multiple_of(i * 1024, 1024), 1024)
            o_copies.append(local(out_w.at[:, columns], w_out.at[i]))

    for copy in own_u:
        copy.wait()
    ua1, ub1 = gather_one(u_all)

    ha2 = ring_two(ha1, lambda i: h_a.at[i, 0:80], lambda i: h_a.at[i, 80:144], x, at_x)
    hb2 = ring_two(hb1, lambda i: h_b.at[i, 0:80], lambda i: h_b.at[i, 80:144], y, at_y)
    z2 = ring_two(
        z1, lambda i: z_all.at[i * 2 + c, 0:64], lambda i: z_all.at[i * 2 + c, 64:128], z, at_z
    )
    up_z, down_z = wrap(z + 1), wrap(z - 1)
    s1 = send(z_all.at[up_z * 2 + c], z_all.at[up_z * 2 + c], sibling)
    s2 = send(z_all.at[down_z * 2 + c], z_all.at[down_z * 2 + c], sibling)

    for copy in w_copies:
        copy.wait()
    acc[...] = jnp.zeros_like(acc)

    def project(i):
        acc[...] += mm(z_all[i], w_all[i])

    def project_near(i, _):
        project(wrap(z + i + i // 2) * 2 + c)
        return 0

    lax.fori_loop(0, 3, project_near, 0)

    da2 = ring_two(da1, lambda i: d_a.at[i, 0:4], lambda i: d_a.at[i, 4:8], y, at_y)
    db2 = ring_two(db1, lambda i: d_b.at[i, 0:4], lambda i: d_b.at[i, 4:8], x, at_x)
    ua2, ub2 = gather_two(u_all, ua1, ub1)

    landed(z2)
    far = wrap(z + 2) * 2 + c
    s3 = send(z_all.at[far], z_all.at[far], sibling)
    landed((s0, s1, s2))

    def project_far(i, _):
        mine = wrap(z + 2) * 2 + c
        theirs = wrap(z + i + i // 2) * 2 + other
        project(jnp.where(i == 3, mine, theirs))
        return 0

    lax.fori_loop(0, 4, project_far, 0)
    landed((s3,))
    project(wrap(z + 2) * 2 + other)

    landed(ha2)
    landed(hb2)

    def ids_of(h):
        return jnp.concatenate(
            [h[i, 128:144, 0:128].astype(F32)[0:1] for i in range(4)], axis=1
        )

    def fold(h, d, ids, j, owner, total):
        rows = h[:, 0:128, :].reshape(512, 512)
        maps = d[j].reshape(384, 512)
        every = lax.dot_general(maps, rows, NT, preferred_element_type=F32)
        every = every.reshape(8, 48, 512)
        first = (owner * 8).astype(F32)
        for i in range(8):
            total = total + jnp.where(ids == first + float(i), every[i], 0.0)
        return total

    ids_a, ids_b = ids_of(h_a), ids_of(h_b)
    zero_low = jnp.zeros((48, 512), F32)

    def near_a(i, total):
        j = wrap(y + i + i // 2)
        return fold(h_a, d_a, ids_a, j, x * 4 + j, total)

    def near_b(i, total):
        j = wrap(x + i + i // 2)
        return fold(h_b, d_b, ids_b, j, j * 4 + y, total)

    low_a = lax.fori_loop(0, 3, near_a, zero_low)
    low_b = lax.fori_loop(0, 3, near_b, zero_low)
    landed(da2)
    low_a = fold(h_a, d_a, ids_a, wrap(y + 2), x * 4 + wrap(y + 2), low_a)
    for i in range(4):
        low_send_a[i] = low_a[:, i * 128 : (i + 1) * 128]
    back_a = [
        send(low_send_a.at[wrap(x + d)], low_recv_a.at[x], at_x(d)) for d in (1, 3, 2)
    ]
    landed(db2)
    low_b = fold(h_b, d_b, ids_b, wrap(x + 2), wrap(x + 2) * 4 + y, low_b)
    for i in range(4):
        low_send_b[i] = low_b[:, i * 128 : (i + 1) * 128]
    back_b = [
        send(low_send_b.at[wrap(y + d)], low_recv_b.at[y], at_y(d)) for d in (1, 3, 2)
    ]

    landed(ua2 + ub2)
    ua3, ub3 = gather_three(u_all)

    landed(back_a)
    landed(back_b)
    part = low_send_a[x] + low_send_b[y]
    for d in (1, 2, 3):
        part = part + low_recv_a[wrap(x + d)] + low_recv_b[wrap(y + d)]
    low_parts[t] = part
    over_t = [
        send(low_parts.at[t], low_parts.at[t], (replica, lax.rem(t + d, 8)))
        for d in range(1, 8)
    ]
    for copy in own_o:
        copy.wait()
    pa1, pb1 = gather_one(p_all)
    oa1, ob1 = gather_one(o_all)
    landed(over_t)

    def spread(low, first):
        source = lax.broadcasted_iota(jnp.int32, (128, 128), 0)
        target = lax.broadcasted_iota(jnp.int32, (128, 128), 1)
        pattern = (source == first + lax.rem(target, 16)).astype(BF16)
        return mm(low, pattern)

    owner_ids = ids_col[...]
    lane_adapter = lax.broadcasted_iota(jnp.int32, (128, 128), 1) // 16

    def expand(tiled):
        return jnp.concatenate(
            [
                jnp.where(owner_ids == lane_adapter + 8 * i, tiled, 0.0).astype(BF16)
                for i in range(16)
            ],
            axis=1,
        )

    low = low_parts[0]
    for i in range(1, 8):
        low = low + low_parts[i]
    low = jnp.concatenate([low, jnp.zeros((80, 128), F32)], axis=0)
    low = jnp.transpose(low, (1, 0)).astype(BF16)

    ua4, ub4 = gather_four(u_all, ua3, ub3)
    expand_q = expand(spread(low, 0))
    expand_k = expand(spread(low, 16))
    expand_v = expand(spread(low, 32))
    landed(ua4 + ub4)

    pa2, pb2 = gather_two(p_all, pa1, pb1)
    oa2, ob2 = gather_two(o_all, oa1, ob1)

    def raised(expanded, maps, lo, hi):
        return mm(expanded, maps[:, :, :, :, lo:hi].reshape(2048, hi - lo))

    acc[:, 0:512] += ADAPTER_SCALE * raised(expand_q, u_all, 0, 512)
    acc[:, 512:640] += ADAPTER_SCALE * raised(expand_k, u_all, 512, 640)
    acc[:, 640:768] += ADAPTER_SCALE * raised(expand_v, u_all, 640, 768)

    landed(pa2 + pb2)
    pa3, pb3 = gather_three(p_all)
    landed(oa2 + ob2)

    def rotated(columns):
        flat = acc[:, columns * 128 : (columns + 1) * 128]
        turned = flat * cosines[...] + pltpu.roll(flat, 64, 1) * sines[...]
        return turned.astype(BF16).astype(F32)

    new_key = rotated(4)
    new_value = acc[:, 640:768].astype(BF16).astype(F32)
    row_lengths = jnp.broadcast_to(lengths[...], (128, 128))
    for i in range(8):
        rows = pl.ds(i, 128, stride=8)
        q_rows[rows, :] = rotated(i % 4)
        key_rows[rows, :] = new_key
        value_rows[rows, :] = new_value
        length_rows[rows, :] = row_lengths

    k_copy.wait()
    v_copy.wait()
    scale = 1.0 / (128.0 ** 0.5)

    def attend(b, _):
        first = pl.multiple_of(b * 128, 128)
        rows = pl.ds(first, 128)
        q = q_rows[rows, :]
        q16 = q.astype(BF16)
        scores = []
        for i in range(16):
            scores.append(
                lax.dot_general(
                    q16[i * 8 : (i + 1) * 8], k_all[b * 16 + i], NT, preferred_element_type=F32
                )
            )
        scores = jnp.concatenate(scores, axis=0) * scale
        self_score = jnp.sum(q * key_rows[rows, :], axis=1, keepdims=True) * scale
        slot = lax.broadcasted_iota(jnp.int32, (128, 128), 1).astype(F32)
        valid = slot < length_rows[rows, :]
        highest = jnp.maximum(
            jnp.max(jnp.where(valid, scores, NEGATIVE), axis=1, keepdims=True), self_score
        )
        weights = jnp.where(valid, jnp.exp(scores - highest), 0.0)
        self_weight = jnp.exp(self_score - highest)
        total = jnp.sum(weights, axis=1, keepdims=True) + self_weight
        weights16 = (weights / total).astype(BF16)
        self16 = (self_weight / total).astype(BF16).astype(F32)
        mixed = []
        for i in range(16):
            mixed.append(mm(weights16[i * 8 : (i + 1) * 8], v_all[b * 16 + i]))
        mixed_rows[rows, :] = jnp.concatenate(mixed, axis=0) + self16 * value_rows[rows, :]
        return 0

    lax.fori_loop(0, 8, attend, 0)
    attended = jnp.concatenate(
        [mixed_rows[pl.ds(i, 128, stride=8), :].astype(BF16) for i in range(4)], axis=1
    )

    pa4, pb4 = gather_four(p_all, pa3, pb3)
    oa3, ob3 = gather_three(o_all)
    landed(pa4 + pb4)
    own_ids = h_a[x, 128:144, 0:128].astype(F32)[0:1]
    low_out = jnp.zeros((16, 128), F32)
    for j in range(4):
        maps = p_all[j].reshape(512, 512)
        every = lax.dot_general(maps, attended, NT, preferred_element_type=F32)
        every = every.reshape(32, 16, 128)
        for i in range(32):
            low_out = low_out + jnp.where(own_ids == float(j * 32 + i), every[i], 0.0)
    out_parts[t] = low_out
    out_over_t = [
        send(out_parts.at[t], out_parts.at[t], (replica, lax.rem(t + d, 8)))
        for d in range(1, 8)
    ]

    for copy in o_copies:
        copy.wait()
    to_sibling = {}
    for d in (2, 1, 3, 0):
        i = wrap(z + d)
        sib_send[i] = mm(attended, w_out[i * 2 + other]).astype(BF16)
        to_sibling[d] = send(sib_send.at[i], sib_recv.at[i], sibling)

    def chip_sum(d):
        i = wrap(z + d)
        mine = mm(attended, w_out[i * 2 + c])
        to_sibling[d].wait_recv()
        return mine + sib_recv[i].astype(F32)

    far_send[...] = chip_sum(2).astype(BF16)
    f1 = send(far_send.at[0:64], far_plus, at_z(1))
    f2 = send(far_send.at[64:128], far_minus, at_z(-1))
    total = chip_sum(1)
    f1.wait_recv()
    near_send[0, 0:64] = (total[0:64] + far_plus[...].astype(F32)).astype(BF16)
    near_send[0, 64:128] = total[64:128].astype(BF16)
    n1 = send(near_send.at[0], near_recv.at[0], at_z(1))
    total = chip_sum(3)
    f2.wait_recv()
    near_send[1, 0:64] = total[0:64].astype(BF16)
    near_send[1, 64:128] = (total[64:128] + far_minus[...].astype(F32)).astype(BF16)
    n2 = send(near_send.at[1], near_recv.at[1], at_z(-1))
    own_sum[...] = chip_sum(0)

    landed(out_over_t)
    low_out = out_parts[0]
    for i in range(1, 8):
        low_out = low_out + out_parts[i]
    low_out = jnp.concatenate([low_out, jnp.zeros((112, 128), F32)], axis=0)
    low_out = jnp.transpose(low_out, (1, 0)).astype(BF16)
    expand_o = expand(spread(low_out, 0))
    oa4, ob4 = gather_four(o_all, oa3, ob3)
    landed((n1, n2))
    own_sum[...] += near_recv[0].astype(F32) + near_recv[1].astype(F32)
    landed(oa4 + ob4)
    out[...] = (own_sum[...] + ADAPTER_SCALE * mm(expand_o, o_all[...].reshape(2048, 1024))).astype(BF16)

    for copy in sent:
        copy.wait_send()


def shards(
    hidden,
    query_weight,
    keyvalue_weight,
    output_weight,
    adapter_down_maps,
    adapter_up_query,
    adapter_up_keyvalue,
    adapter_down_output,
    adapter_up_output,
    cached_keys,
    cached_values,
    context_lengths,
    request_list_slots,
    group_adapter_lists,
):
    group = lax.axis_index("replica")
    wanted = lax.dynamic_index_in_dim(group_adapter_lists, group, 0, keepdims=False)
    chosen = request_list_slots[:, None] == jnp.arange(wanted.shape[0], dtype=jnp.int32)[None, :]
    ids = jnp.sum(jnp.where(chosen, wanted[None, :], 0), axis=1)
    ids_rows = jnp.broadcast_to(jnp.tile(ids, 4)[None, :], (16, 512)).astype(BF16)
    half_size = 64
    frequency = ROPE_BASE ** (-(jnp.arange(half_size, dtype=F32) * 2.0) / 128)
    angles = context_lengths.astype(F32)[:, None] * frequency[None, :]
    cosine, sine = jnp.cos(angles), jnp.sin(angles)
    cosines = jnp.concatenate([cosine, cosine], axis=1)
    sines = jnp.concatenate([-sine, sine], axis=1)
    lengths = context_lengths.astype(F32)[:, None]

    hbm = pl.BlockSpec(memory_space=pl.ANY)
    vmem = pl.BlockSpec(memory_space=pltpu.VMEM)
    return pl.pallas_call(
        kernel,
        out_shape=jax.ShapeDtypeStruct((128, 1024), BF16),
        in_specs=[hbm, hbm, vmem, vmem, vmem, vmem] + [hbm] * 10,
        out_specs=vmem,
        scratch_shapes=[
            pltpu.VMEM((8, 128, 1024), BF16),
            pltpu.VMEM((4, 144, 512), BF16),
            pltpu.VMEM((4, 144, 512), BF16),
            pltpu.VMEM((4, 8, 48, 512), BF16),
            pltpu.VMEM((4, 8, 48, 512), BF16),
            pltpu.VMEM((4, 4, 8, 16, 768), BF16),
            pltpu.VMEM((4, 4, 8, 16, 512), BF16),
            pltpu.VMEM((4, 4, 8, 16, 1024), BF16),
            pltpu.VMEM((8, 1024, 768), BF16),
            pltpu.VMEM((8, 512, 1024), BF16),
            pltpu.VMEM((128, 128, 128), BF16),
            pltpu.VMEM((128, 128, 128), BF16),
            pltpu.VMEM((128, 768), F32),
            pltpu.VMEM((4, 48, 128), F32),
            pltpu.VMEM((4, 48, 128), F32),
            pltpu.VMEM((4, 48, 128), F32),
            pltpu.VMEM((4, 48, 128), F32),
            pltpu.VMEM((8, 48, 128), F32),
            pltpu.VMEM((8, 16, 128), F32),
            pltpu.VMEM((1024, 128), F32),
            pltpu.VMEM((1024, 128), F32),
            pltpu.VMEM((1024, 128), F32),
            pltpu.VMEM((1024, 128), F32),
            pltpu.VMEM((1024, 128), F32),
            pltpu.VMEM((4, 128, 1024), BF16),
            pltpu.VMEM((4, 128, 1024), BF16),
            pltpu.VMEM((128, 1024), BF16),
            pltpu.VMEM((64, 1024), BF16),
            pltpu.VMEM((64, 1024), BF16),
            pltpu.VMEM((2, 128, 1024), BF16),
            pltpu.VMEM((2, 128, 1024), BF16),
            pltpu.VMEM((128, 1024), F32),
            pltpu.SemaphoreType.DMA((SENDS,)),
            pltpu.SemaphoreType.DMA((SENDS,)),
            pltpu.SemaphoreType.DMA((LOCALS,)),
        ],
        compiler_params=pltpu.CompilerParams(
            collective_id=0, has_side_effects=True, vmem_limit_bytes=62 * 1024 * 1024
        ),
        cost_estimate=pl.CostEstimate(flops=8_000_000_000, bytes_accessed=32_000_000, transcendentals=0),
    )(
        hidden,
        ids_rows,
        ids[:, None],
        cosines,
        sines,
        lengths,
        query_weight.reshape(8, 1024, 512),
        keyvalue_weight.reshape(2, 8, 1024, 128),
        output_weight,
        jnp.transpose(adapter_down_maps, (0, 2, 1)),
        adapter_up_query,
        adapter_up_keyvalue,
        jnp.transpose(adapter_down_output, (0, 2, 1)),
        adapter_up_output,
        cached_keys.reshape(128, 128, 128),
        cached_values.reshape(128, 128, 128),
    )


def solution(mesh):
    in_specs = (
        P("replica", "tensor"),
        P(None, "tensor"),
        P(None, None, "tensor"),
        P("tensor", None),
        P("replica", "tensor", None),
        P("replica", None, "tensor"),
        P("replica", None, None, "tensor"),
        P("replica", "tensor", None),
        P("replica", None, "tensor"),
        P("replica", "tensor", None, None),
        P("replica", "tensor", None, None),
        P("replica"),
        P("replica"),
        P(),
    )
    out_specs = P("replica", "tensor")
    return jax.shard_map(shards, mesh=mesh, in_specs=in_specs, out_specs=out_specs, check_vma=False)
```

```python
import functools

import jax
import jax.numpy as jnp
import numpy as np
from jax import lax
from jax.experimental import pallas as pl
from jax.experimental.pallas import tpu as pltpu
from jax.sharding import PartitionSpec as P

ADAPTER_SCALE = 2.0
ROPE_BASE = 500000.0
MESH = pl.DeviceIdType.MESH
BF16 = jnp.bfloat16
F32 = jnp.float32
NT = (((1,), (1,)), ((), ()))
NEGATIVE = -1e30
SENDS = 144
LOCALS = 64


def mm(a, b):
    return jnp.dot(a, b, preferred_element_type=F32)


def kernel(
    hidden, lists, slots, lengths, frequencies,
    query_w, kv_w, out_w, down, up_q, up_kv, down_o, up_o, keys, values,
    out,
    z_all, h_a, h_b, d_a, d_b, u_all, p_all, o_a, o_b, w_all, w_out, k_all, v_all,
    acc, low_send_a, low_recv_a, low_send_b, low_recv_b, low_parts, out_parts,
    q_rows, key_rows, value_rows, length_rows, mixed_rows,
    sib_send, sib_recv, own_sum, lists_v, slots_v, lengths_v, frequencies_v, id_columns_a, id_columns_b,
    low_a, low_b, z_far, z_half, z_near, z_back, x_far, x_half, x_near, x_back, y_far, y_half, y_near, y_back,
    send_sem, recv_sem, local_sem,
):
    replica = lax.axis_index("replica")
    t = lax.axis_index("tensor")
    x, y = replica // 4, replica % 4
    z, c = t // 2, t % 2
    other = 1 - c

    def wrap(v):
        return lax.rem(v + 4, 4)

    def at_x(d):
        return (wrap(x + d) * 4 + y, t)

    def at_y(d):
        return (x * 4 + wrap(y + d), t)

    def at_z(d):
        return (replica, wrap(z + d) * 2 + c)

    sibling = (replica, z * 2 + other)

    counts = {"send": 0, "local": 0}
    sent = []

    def send(src, dst, device):
        i = counts["send"]
        counts["send"] = i + 1
        copy = pltpu.make_async_remote_copy(
            src_ref=src, dst_ref=dst, send_sem=send_sem.at[i], recv_sem=recv_sem.at[i],
            device_id=device, device_id_type=MESH,
        )
        copy.start()
        sent.append(copy)
        return copy

    def local(src, dst):
        i = counts["local"]
        counts["local"] = i + 1
        copy = pltpu.make_async_copy(src, dst, local_sem.at[i])
        copy.start()
        return copy

    barrier = pltpu.get_barrier_semaphore()
    partners = [at_x(d) for d in (1, 2, 3)] + [at_y(d) for d in (1, 2, 3)]
    partners += [(replica, lax.rem(t + d, 8)) for d in range(1, 8)]
    for partner in partners:
        pl.semaphore_signal(barrier, inc=1, device_id=partner, device_id_type=MESH)

    own_small = [local(lists, lists_v), local(slots, slots_v)]
    own_h = [
        local(hidden.at[:, 0:512], h_a.at[x, 0:128]),
        local(hidden.at[:, 512:1024], h_b.at[y, 0:128]),
        local(hidden, z_all.at[t]),
    ]
    own_d = [
        local(down.at[:, :, 0:512], d_a.at[y]),
        local(down.at[:, :, 512:1024], d_b.at[x]),
    ]
    own_u = [
        local(up_q, u_all.at[x, y, :, :, 0:512]),
        local(up_kv.at[:, 0], u_all.at[x, y, :, :, 512:640]),
        local(up_kv.at[:, 1], u_all.at[x, y, :, :, 640:768]),
    ]
    own_p = local(down_o, p_all.at[x, y])
    own_o = [
        local(up_o.at[:, :, 0:512], o_a.at[y]),
        local(up_o.at[:, :, 512:1024], o_b.at[x]),
    ]
    own_late = [local(lengths, lengths_v), local(frequencies, frequencies_v)]

    for copy in own_small:
        copy.wait()
    wanted = lists_v[pl.ds(replica, 1), :].astype(F32).astype(BF16)
    picked = lax.broadcasted_iota(jnp.int32, (32, 128), 0) == slots_v[...]
    own_ids = mm(jnp.broadcast_to(wanted, (16, 32)), picked.astype(F32).astype(BF16))
    id_rows = jnp.concatenate([own_ids] * 4, axis=1).astype(BF16)
    for copy in own_h:
        copy.wait()
    h_a[x, 128:144, :] = id_rows
    h_b[y, 128:144, :] = id_rows
    pl.semaphore_wait(barrier, len(partners))

    arrived = set()

    def landed(copies):
        for copy in copies:
            if id(copy) not in arrived:
                arrived.add(id(copy))
                copy.wait_recv()

    def ring_one(lo, hi, own, device):
        return [
            send(lo(own), lo(own), device(1)),
            send(hi(own), hi(own), device(-1)),
            send(hi(own), hi(own), device(1)),
            send(lo(own), lo(own), device(-1)),
        ]

    def ring_two(first, lo, hi, own, device):
        before, after = wrap(own - 1), wrap(own + 1)
        landed(first[0:1])
        onward = [send(lo(before), lo(before), device(1))]
        landed(first[1:2])
        onward.append(send(hi(after), hi(after), device(-1)))
        return first + onward

    def pool_parts(pool):
        return (
            (lambda i: pool.at[i, y, 0:2], lambda i: pool.at[i, y, 2:4], x, at_x),
            (lambda i: pool.at[x, i, 4:6], lambda i: pool.at[x, i, 6:8], y, at_y),
            (lambda i: pool.at[:, i, 0:2], lambda i: pool.at[:, i, 2:4], y, at_y),
            (lambda i: pool.at[i, :, 4:6], lambda i: pool.at[i, :, 6:8], x, at_x),
        )

    def gather_one(pool):
        parts = pool_parts(pool)
        return ring_one(*parts[0]), ring_one(*parts[1])

    def gather_two(pool, a, b):
        parts = pool_parts(pool)
        return ring_two(a, *parts[0]), ring_two(b, *parts[1])

    def gather_three(pool):
        parts = pool_parts(pool)
        return ring_one(*parts[2]), ring_one(*parts[3])

    def gather_four(pool, a, b):
        parts = pool_parts(pool)
        return ring_two(a, *parts[2]), ring_two(b, *parts[3])

    ha_parts = (lambda i: h_a.at[i, 0:80], lambda i: h_a.at[i, 80:144], x, at_x)
    hb_parts = (lambda i: h_b.at[i, 0:80], lambda i: h_b.at[i, 80:144], y, at_y)
    z_parts = (lambda i: z_all.at[i * 2 + c, 0:64], lambda i: z_all.at[i * 2 + c, 64:128], z, at_z)
    da_parts = (lambda i: d_a.at[i, 0:4], lambda i: d_a.at[i, 4:8], y, at_y)
    db_parts = (lambda i: d_b.at[i, 0:4], lambda i: d_b.at[i, 4:8], x, at_x)
    oa_parts = (lambda i: o_a.at[i, 0:4], lambda i: o_a.at[i, 4:8], y, at_y)
    ob_parts = (lambda i: o_b.at[i, 0:4], lambda i: o_b.at[i, 4:8], x, at_x)

    ha1 = ring_one(*ha_parts)
    hb1 = ring_one(*hb_parts)
    z1 = ring_one(*z_parts)
    s0 = send(z_all.at[t], z_all.at[t], sibling)
    for copy in own_d:
        copy.wait()
    da1 = ring_one(*da_parts)
    db1 = ring_one(*db_parts)

    w_copies = []
    for d in range(8):
        i = lax.rem(t + d, 8)
        w_copies.append(local(query_w.at[i], w_all.at[i, :, 0:512]))
        w_copies.append(local(kv_w.at[0, i], w_all.at[i, :, 512:640]))
        w_copies.append(local(kv_w.at[1, i], w_all.at[i, :, 640:768]))
    k_copy = local(keys, k_all)
    v_copy = local(values, v_all)
    o_copies = []
    for d in (2, 1, 3, 0):
        for core in (other, c):
            i = wrap(z + d) * 2 + core
            columns = pl.ds(pl.multiple_of(i * 1024, 1024), 1024)
            o_copies.append(local(out_w.at[:, columns], w_out.at[i]))

    for copy in own_u:
        copy.wait()
    ua1, ub1 = gather_one(u_all)

    ha2 = ring_two(ha1, *ha_parts)
    hb2 = ring_two(hb1, *hb_parts)
    z2 = ring_two(z1, *z_parts)
    landed(z1)
    up_z, down_z = wrap(z + 1), wrap(z - 1)
    s1 = send(z_all.at[up_z * 2 + c], z_all.at[up_z * 2 + c], sibling)
    s2 = send(z_all.at[down_z * 2 + c], z_all.at[down_z * 2 + c], sibling)

    for copy in w_copies:
        copy.wait()
    acc[...] = jnp.zeros_like(acc)

    def project(i):
        acc[...] += mm(z_all[i], w_all[i])

    def project_near(i, _):
        project(wrap(z + i + i // 2) * 2 + c)
        return 0

    lax.fori_loop(0, 3, project_near, 0)

    for copy in own_late:
        copy.wait()

    def column(row):
        return jnp.transpose(jnp.broadcast_to(row, (128, 128)), (1, 0))

    row_lengths = column(lengths_v[...].astype(F32))
    angles = row_lengths * frequencies_v[...]
    lane = lax.broadcasted_iota(jnp.int32, (128, 128), 1)
    cosines = jnp.cos(angles)
    sines = jnp.where(lane < 64, -jnp.sin(angles), jnp.sin(angles))
    owner_ids = column(own_ids[0:1])

    da2 = ring_two(da1, *da_parts)
    db2 = ring_two(db1, *db_parts)
    ua2, ub2 = gather_two(u_all, ua1, ub1)

    landed(z2)
    far = wrap(z + 2) * 2 + c
    s3 = send(z_all.at[far], z_all.at[far], sibling)
    landed((s0, s1, s2))

    def project_far(i, _):
        mine = wrap(z + 2) * 2 + c
        theirs = wrap(z + i + i // 2) * 2 + other
        project(jnp.where(i == 3, mine, theirs))
        return 0

    lax.fori_loop(0, 4, project_far, 0)
    landed((s3,))
    project(wrap(z + 2) * 2 + other)

    landed(ha2)
    landed(hb2)

    def ids_of(h):
        return jnp.concatenate(
            [h[i, 128:144, 0:128].astype(F32)[0:1] for i in range(4)], axis=1
        )

    def fold(h, d, ids, j, owner, total):
        rows = h[:, 0:128, :].reshape(512, 512)
        maps = d[j].reshape(384, 512)
        every = lax.dot_general(maps, rows, NT, preferred_element_type=F32)
        every = every.reshape(8, 48, 512)
        first = (owner * 8).astype(F32)
        for i in range(8):
            total = total + jnp.where(ids == first + float(i), every[i], 0.0)
        return total

    ids_a, ids_b = ids_of(h_a), ids_of(h_b)
    for i in range(4):
        id_columns_a[i] = column(ids_a[:, i * 128 : (i + 1) * 128])
        id_columns_b[i] = column(ids_b[:, i * 128 : (i + 1) * 128])
    landed(da1)
    landed(db1)
    zero_low = jnp.zeros((48, 512), F32)

    def near_a(i, total):
        j = wrap(y + i + i // 2)
        return fold(h_a, d_a, ids_a, j, x * 4 + j, total)

    def near_b(i, total):
        j = wrap(x + i + i // 2)
        return fold(h_b, d_b, ids_b, j, j * 4 + y, total)

    sum_a = lax.fori_loop(0, 3, near_a, zero_low)
    sum_b = lax.fori_loop(0, 3, near_b, zero_low)
    landed(da2)
    sum_a = fold(h_a, d_a, ids_a, wrap(y + 2), x * 4 + wrap(y + 2), sum_a)
    for i in range(4):
        low_send_a[i] = sum_a[:, i * 128 : (i + 1) * 128]
    back_a = [
        send(low_send_a.at[wrap(x + d)], low_recv_a.at[x], at_x(d)) for d in (1, 3, 2)
    ]
    landed(db2)
    sum_b = fold(h_b, d_b, ids_b, wrap(x + 2), wrap(x + 2) * 4 + y, sum_b)
    for i in range(4):
        low_send_b[i] = sum_b[:, i * 128 : (i + 1) * 128]
    back_b = [
        send(low_send_b.at[wrap(y + d)], low_recv_b.at[y], at_y(d)) for d in (1, 3, 2)
    ]

    landed(ua2 + ub2)
    ua3, ub3 = gather_three(u_all)

    landed(back_a)
    landed(back_b)
    part = low_send_a[x] + low_send_b[y]
    for d in (1, 2, 3):
        part = part + low_recv_a[wrap(x + d)] + low_recv_b[wrap(y + d)]
    low_parts[t] = part
    over_t = [
        send(low_parts.at[t], low_parts.at[t], (replica, lax.rem(t + d, 8)))
        for d in range(1, 8)
    ]
    own_p.wait()
    pa1, pb1 = gather_one(p_all)
    landed(over_t)

    def spread(low, first):
        source = lax.broadcasted_iota(jnp.int32, (128, 128), 0)
        target = lax.broadcasted_iota(jnp.int32, (128, 128), 1)
        pattern = (source == first + lax.rem(target, 16)).astype(BF16)
        return mm(low, pattern)

    lane_adapter = (lane // 16).astype(F32)

    def expand(tiled):
        return jnp.concatenate(
            [
                jnp.where(owner_ids == lane_adapter + 8.0 * i, tiled, 0.0).astype(BF16)
                for i in range(16)
            ],
            axis=1,
        )

    low = low_parts[0]
    for i in range(1, 8):
        low = low + low_parts[i]
    low = jnp.concatenate([low, jnp.zeros((80, 128), F32)], axis=0)
    low = jnp.transpose(low, (1, 0)).astype(BF16)

    ua4, ub4 = gather_four(u_all, ua3, ub3)
    expand_q = expand(spread(low, 0))
    expand_k = expand(spread(low, 16))
    expand_v = expand(spread(low, 32))

    pa2, pb2 = gather_two(p_all, pa1, pb1)
    landed(ua4 + ub4)
    landed(pa2 + pb2)
    pa3, pb3 = gather_three(p_all)
    for copy in own_o:
        copy.wait()
    oa1 = ring_one(*oa_parts)
    ob1 = ring_one(*ob_parts)

    def raised(expanded, maps, lo, hi):
        return mm(expanded, maps[:, :, :, :, lo:hi].reshape(2048, hi - lo))

    acc[:, 0:512] += ADAPTER_SCALE * raised(expand_q, u_all, 0, 512)
    acc[:, 512:640] += ADAPTER_SCALE * raised(expand_k, u_all, 512, 640)
    acc[:, 640:768] += ADAPTER_SCALE * raised(expand_v, u_all, 640, 768)

    def rotated(columns):
        flat = acc[:, columns * 128 : (columns + 1) * 128]
        turned = flat * cosines + pltpu.roll(flat, 64, 1) * sines
        return turned.astype(BF16).astype(F32)

    new_key = rotated(4)
    new_value = acc[:, 640:768].astype(BF16).astype(F32)
    for i in range(8):
        rows = pl.ds(i, 128, stride=8)
        q_rows[rows, :] = rotated(i % 4)
        key_rows[rows, :] = new_key
        value_rows[rows, :] = new_value
        length_rows[rows, :] = row_lengths

    k_copy.wait()
    v_copy.wait()
    scale = 1.0 / (128.0 ** 0.5)

    def attend(b, _):
        first = pl.multiple_of(b * 128, 128)
        rows = pl.ds(first, 128)
        q = q_rows[rows, :]
        q16 = q.astype(BF16)
        scores = []
        for i in range(16):
            scores.append(
                lax.dot_general(
                    q16[i * 8 : (i + 1) * 8], k_all[b * 16 + i], NT, preferred_element_type=F32
                )
            )
        scores = jnp.concatenate(scores, axis=0) * scale
        self_score = jnp.sum(q * key_rows[rows, :], axis=1, keepdims=True) * scale
        slot = lax.broadcasted_iota(jnp.int32, (128, 128), 1).astype(F32)
        valid = slot < length_rows[rows, :]
        highest = jnp.maximum(
            jnp.max(jnp.where(valid, scores, NEGATIVE), axis=1, keepdims=True), self_score
        )
        weights = jnp.where(valid, jnp.exp(scores - highest), 0.0)
        self_weight = jnp.exp(self_score - highest)
        total = jnp.sum(weights, axis=1, keepdims=True) + self_weight
        weights16 = (weights / total).astype(BF16)
        self16 = (self_weight / total).astype(BF16).astype(F32)
        mixed = []
        for i in range(16):
            mixed.append(mm(weights16[i * 8 : (i + 1) * 8], v_all[b * 16 + i]))
        mixed_rows[rows, :] = jnp.concatenate(mixed, axis=0) + self16 * value_rows[rows, :]
        return 0

    lax.fori_loop(0, 4, attend, 0)
    pa4, pb4 = gather_four(p_all, pa3, pb3)
    oa2 = ring_two(oa1, *oa_parts)
    ob2 = ring_two(ob1, *ob_parts)
    lax.fori_loop(4, 8, attend, 0)
    attended = jnp.concatenate(
        [mixed_rows[pl.ds(i, 128, stride=8), :].astype(BF16) for i in range(4)], axis=1
    )

    landed(pa4 + pb4)
    own_row = own_ids[0:1]
    low_out = jnp.zeros((16, 128), F32)
    for j in range(4):
        maps = p_all[j].reshape(512, 512)
        every = lax.dot_general(maps, attended, NT, preferred_element_type=F32)
        every = every.reshape(32, 16, 128)
        for i in range(32):
            low_out = low_out + jnp.where(own_row == float(j * 32 + i), every[i], 0.0)
    out_parts[t] = low_out
    out_over_t = [
        send(out_parts.at[t], out_parts.at[t], (replica, lax.rem(t + d, 8)))
        for d in range(1, 8)
    ]

    for copy in o_copies:
        copy.wait()
    to_sibling = {}
    for d in (2, 1, 3, 0):
        i = wrap(z + d)
        sib_send[i] = mm(attended, w_out[i * 2 + other]).astype(BF16)
        to_sibling[d] = send(sib_send.at[i], sib_recv.at[i], sibling)

    landed(out_over_t)
    low_out = out_parts[0]
    for i in range(1, 8):
        low_out = low_out + out_parts[i]
    low_out = jnp.concatenate([low_out, jnp.zeros((112, 128), F32)], axis=0)
    low_out = jnp.transpose(low_out, (1, 0)).astype(BF16)
    tiled = spread(low_out, 0).astype(BF16)
    low_a[x] = tiled
    low_b[y] = tiled
    around_a = [send(low_a.at[x], low_a.at[x], at_x(d)) for d in (2, 1, 3)]
    around_b = [send(low_b.at[y], low_b.at[y], at_y(d)) for d in (2, 1, 3)]

    def sum_far(block, far, half, device):
        far[...] = block.astype(BF16)
        return [
            send(far.at[0:64], half.at[0], device(1)),
            send(far.at[64:128], half.at[1], device(-1)),
        ]

    def sum_near(block, d, halves, half, near, back, device):
        if d == 1:
            landed(halves[0:1])
            near[0, 0:64] = (block[0:64] + half[0].astype(F32)).astype(BF16)
            near[0, 64:128] = block[64:128].astype(BF16)
            return send(near.at[0], back.at[0], device(1))
        landed(halves[1:2])
        near[1, 0:64] = block[0:64].astype(BF16)
        near[1, 64:128] = (block[64:128] + half[1].astype(F32)).astype(BF16)
        return send(near.at[1], back.at[1], device(-1))

    def chip_sum(d):
        i = wrap(z + d)
        mine = mm(attended, w_out[i * 2 + c])
        landed([to_sibling[d]])
        return mine + sib_recv[i].astype(F32)

    halves = sum_far(chip_sum(2), z_far, z_half, at_z)
    z_plus = sum_near(chip_sum(1), 1, halves, z_half, z_near, z_back, at_z)
    z_minus = sum_near(chip_sum(3), 3, halves, z_half, z_near, z_back, at_z)

    landed(oa2)
    landed(ob2)
    landed(around_a)
    landed(around_b)

    def product(g, columns, lows, owner, maps):
        rows = lows[g].astype(F32)
        blocks = []
        for j in range(4):
            first = (owner(j) * 8).astype(F32)
            blocks.append(jnp.where(columns[g] == lane_adapter + first, rows, 0.0).astype(BF16))
        return ADAPTER_SCALE * mm(jnp.concatenate(blocks, axis=1), maps[...].reshape(512, 512))

    def product_a(d):
        return product(wrap(x + d), id_columns_a, low_a, lambda j: x * 4 + j, o_a)

    def product_b(d):
        return product(wrap(y + d), id_columns_b, low_b, lambda j: j * 4 + y, o_b)

    halves_a = sum_far(product_a(2), x_far, x_half, at_x)
    halves_b = sum_far(product_b(2), y_far, y_half, at_y)
    near_plus_a, near_plus_b = product_a(1), product_b(1)
    x_plus = sum_near(near_plus_a, 1, halves_a, x_half, x_near, x_back, at_x)
    y_plus = sum_near(near_plus_b, 1, halves_b, y_half, y_near, y_back, at_y)
    x_minus = sum_near(product_a(3), 3, halves_a, x_half, x_near, x_back, at_x)
    y_minus = sum_near(product_b(3), 3, halves_b, y_half, y_near, y_back, at_y)
    own_sum[...] = chip_sum(0)
    own_sum[:, 0:512] += product_a(0)
    own_sum[:, 512:1024] += product_b(0)
    landed([z_plus, z_minus])
    own_sum[...] += z_back[0].astype(F32) + z_back[1].astype(F32)
    landed([x_plus, x_minus, y_plus, y_minus])
    out[:, 0:512] = own_sum[:, 0:512] + (x_back[0].astype(F32) + x_back[1].astype(F32))
    out[:, 512:1024] = own_sum[:, 512:1024] + (y_back[0].astype(F32) + y_back[1].astype(F32))

    for copy in sent:
        copy.wait_send()


def shards(
    hidden,
    query_weight,
    keyvalue_weight,
    output_weight,
    adapter_down_maps,
    adapter_up_query,
    adapter_up_keyvalue,
    adapter_down_output,
    adapter_up_output,
    cached_keys,
    cached_values,
    context_lengths,
    request_list_slots,
    group_adapter_lists,
):
    pairs = np.arange(64, dtype=np.float32) * np.float32(2.0) / np.float32(128.0)
    frequency = np.power(np.float32(ROPE_BASE), -pairs).astype(np.float32)
    frequencies = jnp.asarray(np.concatenate([frequency, frequency])[None, :])

    hbm = pl.BlockSpec(memory_space=pl.ANY)
    vmem = pl.BlockSpec(memory_space=pltpu.VMEM)
    result = pl.pallas_call(
        kernel,
        out_shape=jax.ShapeDtypeStruct((128, 1024), F32),
        in_specs=[hbm] * 15,
        out_specs=vmem,
        scratch_shapes=[
            pltpu.VMEM((8, 128, 1024), BF16),
            pltpu.VMEM((4, 144, 512), BF16),
            pltpu.VMEM((4, 144, 512), BF16),
            pltpu.VMEM((4, 8, 48, 512), BF16),
            pltpu.VMEM((4, 8, 48, 512), BF16),
            pltpu.VMEM((4, 4, 8, 16, 768), BF16),
            pltpu.VMEM((4, 4, 8, 16, 512), BF16),
            pltpu.VMEM((4, 8, 16, 512), BF16),
            pltpu.VMEM((4, 8, 16, 512), BF16),
            pltpu.VMEM((8, 1024, 768), BF16),
            pltpu.VMEM((8, 512, 1024), BF16),
            pltpu.VMEM((128, 128, 128), BF16),
            pltpu.VMEM((128, 128, 128), BF16),
            pltpu.VMEM((128, 768), F32),
            pltpu.VMEM((4, 48, 128), F32),
            pltpu.VMEM((4, 48, 128), F32),
            pltpu.VMEM((4, 48, 128), F32),
            pltpu.VMEM((4, 48, 128), F32),
            pltpu.VMEM((8, 48, 128), F32),
            pltpu.VMEM((8, 16, 128), F32),
            pltpu.VMEM((1024, 128), F32),
            pltpu.VMEM((1024, 128), F32),
            pltpu.VMEM((1024, 128), F32),
            pltpu.VMEM((1024, 128), F32),
            pltpu.VMEM((1024, 128), F32),
            pltpu.VMEM((4, 128, 1024), BF16),
            pltpu.VMEM((4, 128, 1024), BF16),
            pltpu.VMEM((128, 1024), F32),
            pltpu.VMEM((16, 32), jnp.int32),
            pltpu.VMEM((1, 128), jnp.int32),
            pltpu.VMEM((1, 128), jnp.int32),
            pltpu.VMEM((1, 128), F32),
            pltpu.VMEM((4, 128, 128), F32),
            pltpu.VMEM((4, 128, 128), F32),
            pltpu.VMEM((4, 128, 128), BF16),
            pltpu.VMEM((4, 128, 128), BF16),
            pltpu.VMEM((128, 1024), BF16),
            pltpu.VMEM((2, 64, 1024), BF16),
            pltpu.VMEM((2, 128, 1024), BF16),
            pltpu.VMEM((2, 128, 1024), BF16),
            pltpu.VMEM((128, 512), BF16),
            pltpu.VMEM((2, 64, 512), BF16),
            pltpu.VMEM((2, 128, 512), BF16),
            pltpu.VMEM((2, 128, 512), BF16),
            pltpu.VMEM((128, 512), BF16),
            pltpu.VMEM((2, 64, 512), BF16),
            pltpu.VMEM((2, 128, 512), BF16),
            pltpu.VMEM((2, 128, 512), BF16),
            pltpu.SemaphoreType.DMA((SENDS,)),
            pltpu.SemaphoreType.DMA((SENDS,)),
            pltpu.SemaphoreType.DMA((LOCALS,)),
        ],
        compiler_params=pltpu.CompilerParams(
            collective_id=0, has_side_effects=True, vmem_limit_bytes=62 * 1024 * 1024
        ),
        cost_estimate=pl.CostEstimate(flops=8_000_000_000, bytes_accessed=32_000_000, transcendentals=0),
    )(
        hidden,
        group_adapter_lists,
        request_list_slots[None, :],
        context_lengths[None, :],
        frequencies,
        query_weight.reshape(8, 1024, 512),
        keyvalue_weight.reshape(2, 8, 1024, 128),
        output_weight,
        jnp.transpose(adapter_down_maps, (0, 2, 1)),
        adapter_up_query,
        adapter_up_keyvalue,
        jnp.transpose(adapter_down_output, (0, 2, 1)),
        adapter_up_output,
        cached_keys.reshape(128, 128, 128),
        cached_values.reshape(128, 128, 128),
    )
    return result.astype(BF16)


def solution(mesh):
    in_specs = (
        P("replica", "tensor"),
        P(None, "tensor"),
        P(None, None, "tensor"),
        P("tensor", None),
        P("replica", "tensor", None),
        P("replica", None, "tensor"),
        P("replica", None, None, "tensor"),
        P("replica", "tensor", None),
        P("replica", None, "tensor"),
        P("replica", "tensor", None, None),
        P("replica", "tensor", None, None),
        P("replica"),
        P("replica"),
        P(),
    )
    out_specs = P("replica", "tensor")
    return jax.shard_map(shards, mesh=mesh, in_specs=in_specs, out_specs=out_specs, check_vma=False)
```

```python
import functools

import jax
import jax.numpy as jnp
import numpy as np
from jax import lax
from jax.experimental import pallas as pl
from jax.experimental.pallas import tpu as pltpu
from jax.sharding import PartitionSpec as P

ADAPTER_SCALE = 2.0
ROPE_BASE = 500000.0
MESH = pl.DeviceIdType.MESH
BF16 = jnp.bfloat16
F32 = jnp.float32
NT = (((1,), (1,)), ((), ()))
NEGATIVE = -1e30
SENDS = 160
LOCALS = 64


def mm(a, b):
    return jnp.dot(a, b, preferred_element_type=F32)


def kernel(
    hidden, lists, slots, lengths, frequencies,
    query_w, kv_w, out_w, down, up_q, up_kv, down_o, up_o, keys, values,
    out,
    z_all, h_a, h_b, d_a, d_b, u_a, u_b, p_all, o_a, o_b, w_all, w_out, k_all, v_all,
    acc, low_send_a, low_recv_a, low_send_b, low_recv_b, low_parts, out_parts,
    low_mine, low_theirs, out_mine, out_theirs,
    q_rows, key_rows, value_rows, length_rows, mixed_rows,
    sib_send, sib_recv, own_sum, lists_v, slots_v, lengths_v, frequencies_v, id_columns_a, id_columns_b,
    low_a, low_b, out_low_a, out_low_b, *sums,
):
    (
        z_far, z_half, z_near, z_back, x_far, x_half, x_near, x_back, y_far, y_half, y_near, y_back,
        xu_far, xu_half, xu_near, xu_back, yu_far, yu_half, yu_near, yu_back,
        send_sem, recv_sem, local_sem,
    ) = sums
    replica = lax.axis_index("replica")
    t = lax.axis_index("tensor")
    x, y = replica // 4, replica % 4
    z, c = t // 2, t % 2
    other = 1 - c

    def wrap(v):
        return lax.rem(v + 4, 4)

    def at_x(d):
        return (wrap(x + d) * 4 + y, t)

    def at_y(d):
        return (x * 4 + wrap(y + d), t)

    def at_z(d):
        return (replica, wrap(z + d) * 2 + c)

    sibling = (replica, z * 2 + other)

    counts = {"send": 0, "local": 0}
    sent = []

    def send(src, dst, device):
        i = counts["send"]
        counts["send"] = i + 1
        copy = pltpu.make_async_remote_copy(
            src_ref=src, dst_ref=dst, send_sem=send_sem.at[i], recv_sem=recv_sem.at[i],
            device_id=device, device_id_type=MESH,
        )
        copy.start()
        sent.append(copy)
        return copy

    def local(src, dst):
        i = counts["local"]
        counts["local"] = i + 1
        copy = pltpu.make_async_copy(src, dst, local_sem.at[i])
        copy.start()
        return copy

    barrier = pltpu.get_barrier_semaphore()
    partners = [at_x(d) for d in (1, 2, 3)] + [at_y(d) for d in (1, 2, 3)]
    partners += [at_z(d) for d in (1, 2, 3)] + [sibling]
    for partner in partners:
        pl.semaphore_signal(barrier, inc=1, device_id=partner, device_id_type=MESH)

    own_small = [local(lists, lists_v), local(slots, slots_v)]
    own_h = [
        local(hidden.at[:, 0:512], h_a.at[x, 0:128]),
        local(hidden.at[:, 512:1024], h_b.at[y, 0:128]),
        local(hidden, z_all.at[t]),
    ]
    own_d = [
        local(down.at[:, :, 0:512], d_a.at[y]),
        local(down.at[:, :, 512:1024], d_b.at[x]),
    ]
    own_u = [
        local(up_q.at[:, :, 0:256], u_a.at[y, :, :, 0:256]),
        local(up_kv.at[:, 0], u_a.at[y, :, :, 256:384]),
        local(up_q.at[:, :, 256:512], u_b.at[x, :, :, 0:256]),
        local(up_kv.at[:, 1], u_b.at[x, :, :, 256:384]),
    ]
    own_p = local(down_o, p_all.at[x, y])
    own_o = [
        local(up_o.at[:, :, 0:512], o_a.at[y]),
        local(up_o.at[:, :, 512:1024], o_b.at[x]),
    ]
    own_late = [local(lengths, lengths_v), local(frequencies, frequencies_v)]

    for copy in own_small:
        copy.wait()
    wanted = lists_v[pl.ds(replica, 1), :].astype(F32).astype(BF16)
    picked = lax.broadcasted_iota(jnp.int32, (32, 128), 0) == slots_v[...]
    own_ids = mm(jnp.broadcast_to(wanted, (16, 32)), picked.astype(F32).astype(BF16))
    id_rows = jnp.concatenate([own_ids] * 4, axis=1).astype(BF16)
    for copy in own_h:
        copy.wait()
    h_a[x, 128:144, :] = id_rows
    h_b[y, 128:144, :] = id_rows
    pl.semaphore_wait(barrier, len(partners))

    arrived = set()

    def landed(copies):
        for copy in copies:
            if id(copy) not in arrived:
                arrived.add(id(copy))
                copy.wait_recv()

    def ring_one(lo, hi, own, device):
        return [
            send(lo(own), lo(own), device(1)),
            send(hi(own), hi(own), device(-1)),
            send(hi(own), hi(own), device(1)),
            send(lo(own), lo(own), device(-1)),
        ]

    def ring_two(first, lo, hi, own, device):
        before, after = wrap(own - 1), wrap(own + 1)
        landed(first[0:1])
        onward = [send(lo(before), lo(before), device(1))]
        landed(first[1:2])
        onward.append(send(hi(after), hi(after), device(-1)))
        return first + onward

    def pool_parts(pool):
        return (
            (lambda i: pool.at[i, y, 0:2], lambda i: pool.at[i, y, 2:4], x, at_x),
            (lambda i: pool.at[x, i, 4:6], lambda i: pool.at[x, i, 6:8], y, at_y),
            (lambda i: pool.at[:, i, 0:2], lambda i: pool.at[:, i, 2:4], y, at_y),
            (lambda i: pool.at[i, :, 4:6], lambda i: pool.at[i, :, 6:8], x, at_x),
        )

    def gather_one(pool):
        parts = pool_parts(pool)
        return ring_one(*parts[0]), ring_one(*parts[1])

    def gather_two(pool, a, b):
        parts = pool_parts(pool)
        return ring_two(a, *parts[0]), ring_two(b, *parts[1])

    def gather_three(pool):
        parts = pool_parts(pool)
        return ring_one(*parts[2]), ring_one(*parts[3])

    def gather_four(pool, a, b):
        parts = pool_parts(pool)
        return ring_two(a, *parts[2]), ring_two(b, *parts[3])

    ha_parts = (lambda i: h_a.at[i, 0:80], lambda i: h_a.at[i, 80:144], x, at_x)
    hb_parts = (lambda i: h_b.at[i, 0:80], lambda i: h_b.at[i, 80:144], y, at_y)
    z_parts = (lambda i: z_all.at[i * 2 + c, 0:64], lambda i: z_all.at[i * 2 + c, 64:128], z, at_z)
    da_parts = (lambda i: d_a.at[i, 0:4], lambda i: d_a.at[i, 4:8], y, at_y)
    db_parts = (lambda i: d_b.at[i, 0:4], lambda i: d_b.at[i, 4:8], x, at_x)
    ua_parts = (lambda i: u_a.at[i, 0:4], lambda i: u_a.at[i, 4:8], y, at_y)
    ub_parts = (lambda i: u_b.at[i, 0:4], lambda i: u_b.at[i, 4:8], x, at_x)
    oa_parts = (lambda i: o_a.at[i, 0:4], lambda i: o_a.at[i, 4:8], y, at_y)
    ob_parts = (lambda i: o_b.at[i, 0:4], lambda i: o_b.at[i, 4:8], x, at_x)

    ha1 = ring_one(*ha_parts)
    hb1 = ring_one(*hb_parts)
    z1 = ring_one(*z_parts)
    s0 = send(z_all.at[t], z_all.at[t], sibling)
    for copy in own_d:
        copy.wait()
    da1 = ring_one(*da_parts)
    db1 = ring_one(*db_parts)

    w_copies = []
    for d in range(8):
        i = lax.rem(t + d, 8)
        w_copies.append(local(query_w.at[i], w_all.at[i, :, 0:512]))
        w_copies.append(local(kv_w.at[0, i], w_all.at[i, :, 512:640]))
        w_copies.append(local(kv_w.at[1, i], w_all.at[i, :, 640:768]))
    k_copy = local(keys, k_all)
    v_copy = local(values, v_all)
    o_copies = []
    for d in (2, 1, 3, 0):
        for core in (other, c):
            i = wrap(z + d) * 2 + core
            columns = pl.ds(pl.multiple_of(i * 1024, 1024), 1024)
            o_copies.append(local(out_w.at[:, columns], w_out.at[i]))

    ha2 = ring_two(ha1, *ha_parts)
    hb2 = ring_two(hb1, *hb_parts)
    z2 = ring_two(z1, *z_parts)
    landed(z1)
    up_z, down_z = wrap(z + 1), wrap(z - 1)
    s1 = send(z_all.at[up_z * 2 + c], z_all.at[up_z * 2 + c], sibling)
    s2 = send(z_all.at[down_z * 2 + c], z_all.at[down_z * 2 + c], sibling)
    da2 = ring_two(da1, *da_parts)
    db2 = ring_two(db1, *db_parts)

    for copy in w_copies:
        copy.wait()
    acc[...] = jnp.zeros_like(acc)

    def project(i):
        acc[...] += mm(z_all[i], w_all[i])

    def project_near(i, _):
        project(wrap(z + i + i // 2) * 2 + c)
        return 0

    lax.fori_loop(0, 3, project_near, 0)

    for copy in own_late:
        copy.wait()

    def column(row):
        return jnp.transpose(jnp.broadcast_to(row, (128, 128)), (1, 0))

    row_lengths = column(lengths_v[...].astype(F32))
    angles = row_lengths * frequencies_v[...]
    lane = lax.broadcasted_iota(jnp.int32, (128, 128), 1)
    cosines = jnp.cos(angles)
    sines = jnp.where(lane < 64, -jnp.sin(angles), jnp.sin(angles))
    owner_ids = column(own_ids[0:1])


    landed(z2)
    far = wrap(z + 2) * 2 + c
    s3 = send(z_all.at[far], z_all.at[far], sibling)
    landed((s0, s1, s2))

    def project_far(i, _):
        mine = wrap(z + 2) * 2 + c
        theirs = wrap(z + i + i // 2) * 2 + other
        project(jnp.where(i == 3, mine, theirs))
        return 0

    lax.fori_loop(0, 4, project_far, 0)
    landed((s3,))
    project(wrap(z + 2) * 2 + other)

    landed(ha2)
    landed(hb2)

    def ids_of(h):
        return jnp.concatenate(
            [h[i, 128:144, 0:128].astype(F32)[0:1] for i in range(4)], axis=1
        )

    def fold(h, d, ids, j, owner, total):
        rows = h[:, 0:128, :].reshape(512, 512)
        maps = d[j].reshape(384, 512)
        every = lax.dot_general(maps, rows, NT, preferred_element_type=F32)
        every = every.reshape(8, 48, 512)
        first = (owner * 8).astype(F32)
        for i in range(8):
            total = total + jnp.where(ids == first + float(i), every[i], 0.0)
        return total

    ids_a, ids_b = ids_of(h_a), ids_of(h_b)
    for i in range(4):
        id_columns_a[i] = column(ids_a[:, i * 128 : (i + 1) * 128])
        id_columns_b[i] = column(ids_b[:, i * 128 : (i + 1) * 128])
    landed(da1)
    landed(db1)
    zero_low = jnp.zeros((48, 512), F32)

    def near_a(i, total):
        j = wrap(y + i + i // 2)
        return fold(h_a, d_a, ids_a, j, x * 4 + j, total)

    def near_b(i, total):
        j = wrap(x + i + i // 2)
        return fold(h_b, d_b, ids_b, j, j * 4 + y, total)

    sum_a = lax.fori_loop(0, 3, near_a, zero_low)
    sum_b = lax.fori_loop(0, 3, near_b, zero_low)
    landed(da2)
    sum_a = fold(h_a, d_a, ids_a, wrap(y + 2), x * 4 + wrap(y + 2), sum_a)
    for i in range(4):
        low_send_a[i] = sum_a[:, i * 128 : (i + 1) * 128]
    back_a = [
        send(low_send_a.at[wrap(x + d)], low_recv_a.at[x], at_x(d)) for d in (1, 3, 2)
    ]
    landed(db2)
    sum_b = fold(h_b, d_b, ids_b, wrap(x + 2), wrap(x + 2) * 4 + y, sum_b)
    for i in range(4):
        low_send_b[i] = sum_b[:, i * 128 : (i + 1) * 128]
    back_b = [
        send(low_send_b.at[wrap(y + d)], low_recv_b.at[y], at_y(d)) for d in (1, 3, 2)
    ]

    for copy in own_u:
        copy.wait()
    ua1 = ring_one(*ua_parts)
    ub1 = ring_one(*ub_parts)
    own_p.wait()
    pa1, pb1 = gather_one(p_all)
    landed(back_a)
    landed(back_b)
    part = low_send_a[x] + low_send_b[y]
    for d in (1, 2, 3):
        part = part + low_recv_a[wrap(x + d)] + low_recv_b[wrap(y + d)]
    def over_tensor(part, mine, theirs, parts, forward):
        mine[...] = part
        landed([send(mine, theirs, sibling)])
        parts[z] = part + theirs[...]
        copies = [send(parts.at[z], parts.at[z], at_z(d)) for d in (2, 1, 3)]
        forward()
        landed(copies)
        return (parts[0] + parts[1]) + (parts[2] + parts[3])

    pools = []

    def forward_pools():
        pools.append(ring_two(ua1, *ua_parts))
        pools.append(ring_two(ub1, *ub_parts))
        pools.extend(gather_two(p_all, pa1, pb1))

    low = over_tensor(part, low_mine, low_theirs, low_parts, forward_pools)
    ua2, ub2, pa2, pb2 = pools

    def spread(low, first):
        source = lax.broadcasted_iota(jnp.int32, (128, 128), 0)
        target = lax.broadcasted_iota(jnp.int32, (128, 128), 1)
        pattern = (source == first + lax.rem(target, 16)).astype(F32).astype(BF16)
        return mm(low, pattern)

    lane_adapter = (lane // 16).astype(F32)

    def turned(low):
        padding = jnp.zeros((128 - low.shape[0], 128), F32)
        full = jnp.concatenate([low.astype(F32), padding], axis=0)
        return jnp.transpose(full, (1, 0)).astype(BF16)

    class RingSum:
        def __init__(self, far, half, near, back, device):
            self.far_block, self.half, self.near_block, self.back = far, half, near, back
            self.device = device

        def far(self, block):
            self.far_block[...] = block.astype(BF16)
            self.halves = [
                send(self.far_block.at[0:64], self.half.at[0], self.device(1)),
                send(self.far_block.at[64:128], self.half.at[1], self.device(-1)),
            ]

        def near(self, plus, minus):
            near, back = self.near_block, self.back
            self.waiting = plus[0:64], minus[64:128]
            near[0, 64:128] = plus[64:128].astype(BF16)
            near[1, 0:64] = minus[0:64].astype(BF16)
            self.blocks = [
                send(near.at[0, 64:128], back.at[0, 64:128], self.device(1)),
                send(near.at[1, 0:64], back.at[1, 0:64], self.device(-1)),
            ]

        def join(self):
            near, back = self.near_block, self.back
            landed(self.halves[0:1])
            near[0, 0:64] = (self.waiting[0] + self.half[0].astype(F32)).astype(BF16)
            self.blocks.append(send(near.at[0, 0:64], back.at[0, 0:64], self.device(1)))
            landed(self.halves[1:2])
            near[1, 64:128] = (self.waiting[1] + self.half[1].astype(F32)).astype(BF16)
            self.blocks.append(send(near.at[1, 64:128], back.at[1, 64:128], self.device(-1)))

        def total(self):
            landed(self.blocks)
            return self.back[0].astype(F32) + self.back[1].astype(F32)

    def expand(g, columns, rows, owner):
        blocks = []
        for j in range(4):
            first = (owner(j) * 8).astype(F32)
            blocks.append(jnp.where(columns[g] == lane_adapter + first, rows, 0.0).astype(BF16))
        return jnp.concatenate(blocks, axis=1)

    def owner_a(j):
        return x * 4 + j

    def owner_b(j):
        return j * 4 + y

    low_a[x] = low.astype(BF16)
    low_b[y] = low.astype(BF16)
    around_a = [send(low_a.at[x], low_a.at[x], at_x(d)) for d in (2, 1, 3)]
    around_b = [send(low_b.at[y], low_b.at[y], at_y(d)) for d in (2, 1, 3)]
    landed(ua2)
    landed(ub2)

    def raised(g, columns, lows, first, owner, maps):
        rows = turned(lows[g])
        for_q = expand(g, columns, spread(rows, 0), owner)
        for_kv = expand(g, columns, spread(rows, first), owner)
        return ADAPTER_SCALE * jnp.concatenate(
            [
                mm(for_q, maps[:, :, :, 0:256].reshape(512, 256)),
                mm(for_kv, maps[:, :, :, 256:384].reshape(512, 128)),
            ],
            axis=1,
        )

    def raised_a(d):
        return raised(wrap(x + d), id_columns_a, low_a, 16, owner_a, u_a)

    def raised_b(d):
        return raised(wrap(y + d), id_columns_b, low_b, 32, owner_b, u_b)

    xu = RingSum(xu_far, xu_half, xu_near, xu_back, at_x)
    yu = RingSum(yu_far, yu_half, yu_near, yu_back, at_y)
    landed(around_a[0:1])
    xu.far(raised_a(2))
    landed(around_b[0:1])
    yu.far(raised_b(2))
    landed(around_a)
    xu.near(raised_a(1), raised_a(3))
    landed(around_b)
    yu.near(raised_b(1), raised_b(3))
    own_a, own_b = raised_a(0), raised_b(0)
    xu.join()
    yu.join()
    landed(pa2 + pb2)
    pa3, pb3 = gather_three(p_all)
    for copy in own_o:
        copy.wait()
    own_a = own_a + xu.total()
    acc[:, 0:256] += own_a[:, 0:256]
    acc[:, 512:640] += own_a[:, 256:384]
    own_b = own_b + yu.total()
    acc[:, 256:512] += own_b[:, 0:256]
    acc[:, 640:768] += own_b[:, 256:384]

    def rotated(columns):
        flat = acc[:, columns * 128 : (columns + 1) * 128]
        moved = flat * cosines + pltpu.roll(flat, 64, 1) * sines
        return moved.astype(BF16).astype(F32)

    new_key = rotated(4)
    new_value = acc[:, 640:768].astype(BF16).astype(F32)
    for i in range(8):
        rows = pl.ds(i, 128, stride=8)
        q_rows[rows, :] = rotated(i % 4)
        key_rows[rows, :] = new_key
        value_rows[rows, :] = new_value
        length_rows[rows, :] = row_lengths

    k_copy.wait()
    v_copy.wait()
    scale = 1.0 / (128.0 ** 0.5)

    def attend(b, _):
        first = pl.multiple_of(b * 128, 128)
        rows = pl.ds(first, 128)
        q = q_rows[rows, :]
        q16 = q.astype(BF16)
        scores = []
        for i in range(16):
            scores.append(
                lax.dot_general(
                    q16[i * 8 : (i + 1) * 8], k_all[b * 16 + i], NT, preferred_element_type=F32
                )
            )
        scores = jnp.concatenate(scores, axis=0) * scale
        self_score = jnp.sum(q * key_rows[rows, :], axis=1, keepdims=True) * scale
        slot = lax.broadcasted_iota(jnp.int32, (128, 128), 1).astype(F32)
        valid = slot < length_rows[rows, :]
        highest = jnp.maximum(
            jnp.max(jnp.where(valid, scores, NEGATIVE), axis=1, keepdims=True), self_score
        )
        weights = jnp.where(valid, jnp.exp(scores - highest), 0.0)
        self_weight = jnp.exp(self_score - highest)
        total = jnp.sum(weights, axis=1, keepdims=True) + self_weight
        weights16 = (weights / total).astype(BF16)
        self16 = (self_weight / total).astype(BF16).astype(F32)
        mixed = []
        for i in range(16):
            mixed.append(mm(weights16[i * 8 : (i + 1) * 8], v_all[b * 16 + i]))
        mixed_rows[rows, :] = jnp.concatenate(mixed, axis=0) + self16 * value_rows[rows, :]
        return 0

    lax.fori_loop(0, 3, attend, 0)
    pa4, pb4 = gather_four(p_all, pa3, pb3)
    oa1 = ring_one(*oa_parts)
    ob1 = ring_one(*ob_parts)
    lax.fori_loop(3, 8, attend, 0)
    oa2 = ring_two(oa1, *oa_parts)
    ob2 = ring_two(ob1, *ob_parts)
    attended = jnp.concatenate(
        [mixed_rows[pl.ds(i, 128, stride=8), :].astype(BF16) for i in range(4)], axis=1
    )

    landed(pa4 + pb4)
    own_row = own_ids[0:1]
    low_out = jnp.zeros((16, 128), F32)
    for j in range(4):
        maps = p_all[j].reshape(512, 512)
        every = lax.dot_general(maps, attended, NT, preferred_element_type=F32)
        every = every.reshape(32, 16, 128)
        for i in range(32):
            low_out = low_out + jnp.where(own_row == float(j * 32 + i), every[i], 0.0)
    out_mine[...] = low_out
    to_core = send(out_mine, out_theirs, sibling)

    for copy in o_copies:
        copy.wait()
    to_sibling = {}
    for d in (2, 1, 3, 0):
        i = wrap(z + d)
        sib_send[i] = mm(attended, w_out[i * 2 + other]).astype(BF16)
        to_sibling[d] = send(sib_send.at[i], sib_recv.at[i], sibling)

    def chip_sum(d):
        i = wrap(z + d)
        mine = mm(attended, w_out[i * 2 + c])
        landed([to_sibling[d]])
        return mine + sib_recv[i].astype(F32)

    landed([to_core])
    out_parts[z] = out_mine[...] + out_theirs[...]
    out_over_z = [send(out_parts.at[z], out_parts.at[z], at_z(d)) for d in (2, 1, 3)]
    over_z = RingSum(z_far, z_half, z_near, z_back, at_z)
    over_z.far(chip_sum(2))
    over_z.near(chip_sum(1), chip_sum(3))

    landed(out_over_z)
    low_out = (out_parts[0] + out_parts[1]) + (out_parts[2] + out_parts[3])
    out_low_a[x] = low_out.astype(BF16)
    out_low_b[y] = low_out.astype(BF16)
    around_a = [send(out_low_a.at[x], out_low_a.at[x], at_x(d)) for d in (2, 1, 3)]
    around_b = [send(out_low_b.at[y], out_low_b.at[y], at_y(d)) for d in (2, 1, 3)]
    over_z.join()

    def product(g, columns, lows, owner, maps):
        expanded = expand(g, columns, spread(turned(lows[g]), 0), owner)
        return ADAPTER_SCALE * mm(expanded, maps[...].reshape(512, 512))

    def product_a(d):
        return product(wrap(x + d), id_columns_a, out_low_a, owner_a, o_a)

    def product_b(d):
        return product(wrap(y + d), id_columns_b, out_low_b, owner_b, o_b)

    landed(oa2)
    landed(ob2)
    over_x = RingSum(x_far, x_half, x_near, x_back, at_x)
    over_y = RingSum(y_far, y_half, y_near, y_back, at_y)
    landed(around_a[0:1])
    over_x.far(product_a(2))
    landed(around_b[0:1])
    over_y.far(product_b(2))
    landed(around_a)
    over_x.near(product_a(1), product_a(3))
    landed(around_b)
    over_y.near(product_b(1), product_b(3))
    over_x.join()
    over_y.join()
    own_sum[...] = chip_sum(0)
    own_sum[:, 0:512] += product_a(0)
    own_sum[:, 512:1024] += product_b(0)
    own_sum[...] += over_z.total()
    out[:, 0:512] = own_sum[:, 0:512] + over_x.total()
    out[:, 512:1024] = own_sum[:, 512:1024] + over_y.total()

    for copy in sent:
        copy.wait_send()


def shards(
    hidden,
    query_weight,
    keyvalue_weight,
    output_weight,
    adapter_down_maps,
    adapter_up_query,
    adapter_up_keyvalue,
    adapter_down_output,
    adapter_up_output,
    cached_keys,
    cached_values,
    context_lengths,
    request_list_slots,
    group_adapter_lists,
):
    pairs = np.arange(64, dtype=np.float32) * np.float32(2.0) / np.float32(128.0)
    frequency = np.power(np.float32(ROPE_BASE), -pairs).astype(np.float32)
    frequencies = jnp.asarray(np.concatenate([frequency, frequency])[None, :])

    hbm = pl.BlockSpec(memory_space=pl.ANY)
    vmem = pl.BlockSpec(memory_space=pltpu.VMEM)
    result = pl.pallas_call(
        kernel,
        out_shape=jax.ShapeDtypeStruct((128, 1024), F32),
        in_specs=[hbm] * 15,
        out_specs=vmem,
        scratch_shapes=[
            pltpu.VMEM((8, 128, 1024), BF16),
            pltpu.VMEM((4, 144, 512), BF16),
            pltpu.VMEM((4, 144, 512), BF16),
            pltpu.VMEM((4, 8, 48, 512), BF16),
            pltpu.VMEM((4, 8, 48, 512), BF16),
            pltpu.VMEM((4, 8, 16, 384), BF16),
            pltpu.VMEM((4, 8, 16, 384), BF16),
            pltpu.VMEM((4, 4, 8, 16, 512), BF16),
            pltpu.VMEM((4, 8, 16, 512), BF16),
            pltpu.VMEM((4, 8, 16, 512), BF16),
            pltpu.VMEM((8, 1024, 768), BF16),
            pltpu.VMEM((8, 512, 1024), BF16),
            pltpu.VMEM((128, 128, 128), BF16),
            pltpu.VMEM((128, 128, 128), BF16),
            pltpu.VMEM((128, 768), F32),
            pltpu.VMEM((4, 48, 128), F32),
            pltpu.VMEM((4, 48, 128), F32),
            pltpu.VMEM((4, 48, 128), F32),
            pltpu.VMEM((4, 48, 128), F32),
            pltpu.VMEM((4, 48, 128), F32),
            pltpu.VMEM((4, 16, 128), F32),
            pltpu.VMEM((48, 128), F32),
            pltpu.VMEM((48, 128), F32),
            pltpu.VMEM((16, 128), F32),
            pltpu.VMEM((16, 128), F32),
            pltpu.VMEM((1024, 128), F32),
            pltpu.VMEM((1024, 128), F32),
            pltpu.VMEM((1024, 128), F32),
            pltpu.VMEM((1024, 128), F32),
            pltpu.VMEM((1024, 128), F32),
            pltpu.VMEM((4, 128, 1024), BF16),
            pltpu.VMEM((4, 128, 1024), BF16),
            pltpu.VMEM((128, 1024), F32),
            pltpu.VMEM((16, 32), jnp.int32),
            pltpu.VMEM((1, 128), jnp.int32),
            pltpu.VMEM((1, 128), jnp.int32),
            pltpu.VMEM((1, 128), F32),
            pltpu.VMEM((4, 128, 128), F32),
            pltpu.VMEM((4, 128, 128), F32),
            pltpu.VMEM((4, 48, 128), BF16),
            pltpu.VMEM((4, 48, 128), BF16),
            pltpu.VMEM((4, 16, 128), BF16),
            pltpu.VMEM((4, 16, 128), BF16),
            pltpu.VMEM((128, 1024), BF16),
            pltpu.VMEM((2, 64, 1024), BF16),
            pltpu.VMEM((2, 128, 1024), BF16),
            pltpu.VMEM((2, 128, 1024), BF16),
            pltpu.VMEM((128, 512), BF16),
            pltpu.VMEM((2, 64, 512), BF16),
            pltpu.VMEM((2, 128, 512), BF16),
            pltpu.VMEM((2, 128, 512), BF16),
            pltpu.VMEM((128, 512), BF16),
            pltpu.VMEM((2, 64, 512), BF16),
            pltpu.VMEM((2, 128, 512), BF16),
            pltpu.VMEM((2, 128, 512), BF16),
            pltpu.VMEM((128, 384), BF16),
            pltpu.VMEM((2, 64, 384), BF16),
            pltpu.VMEM((2, 128, 384), BF16),
            pltpu.VMEM((2, 128, 384), BF16),
            pltpu.VMEM((128, 384), BF16),
            pltpu.VMEM((2, 64, 384), BF16),
            pltpu.VMEM((2, 128, 384), BF16),
            pltpu.VMEM((2, 128, 384), BF16),
            pltpu.SemaphoreType.DMA((SENDS,)),
            pltpu.SemaphoreType.DMA((SENDS,)),
            pltpu.SemaphoreType.DMA((LOCALS,)),
        ],
        compiler_params=pltpu.CompilerParams(
            collective_id=0, has_side_effects=True, vmem_limit_bytes=62 * 1024 * 1024
        ),
        cost_estimate=pl.CostEstimate(flops=8_000_000_000, bytes_accessed=32_000_000, transcendentals=0),
    )(
        hidden,
        group_adapter_lists,
        request_list_slots[None, :],
        context_lengths[None, :],
        frequencies,
        query_weight.reshape(8, 1024, 512),
        keyvalue_weight.reshape(2, 8, 1024, 128),
        output_weight,
        jnp.transpose(adapter_down_maps, (0, 2, 1)),
        adapter_up_query,
        adapter_up_keyvalue,
        jnp.transpose(adapter_down_output, (0, 2, 1)),
        adapter_up_output,
        cached_keys.reshape(128, 128, 128),
        cached_values.reshape(128, 128, 128),
    )
    return result.astype(BF16)


def solution(mesh):
    in_specs = (
        P("replica", "tensor"),
        P(None, "tensor"),
        P(None, None, "tensor"),
        P("tensor", None),
        P("replica", "tensor", None),
        P("replica", None, "tensor"),
        P("replica", None, None, "tensor"),
        P("replica", "tensor", None),
        P("replica", None, "tensor"),
        P("replica", "tensor", None, None),
        P("replica", "tensor", None, None),
        P("replica"),
        P("replica"),
        P(),
    )
    out_specs = P("replica", "tensor")
    return jax.shard_map(shards, mesh=mesh, in_specs=in_specs, out_specs=out_specs, check_vma=False)
```

```python
import functools

import jax
import jax.numpy as jnp
import numpy as np
from jax import lax
from jax.experimental import pallas as pl
from jax.experimental.pallas import tpu as pltpu
from jax.sharding import PartitionSpec as P

ADAPTER_SCALE = 2.0
ROPE_BASE = 500000.0
MESH = pl.DeviceIdType.MESH
BF16 = jnp.bfloat16
F32 = jnp.float32
NT = (((1,), (1,)), ((), ()))
NEGATIVE = -1e30
SENDS = 160
LOCALS = 64


def mm(a, b):
    return jnp.dot(a, b, preferred_element_type=F32)


def kernel(
    hidden, lists, slots, lengths, frequencies,
    query_w, kv_w, out_w, down, up_q, up_kv, down_o, up_o, keys, values,
    out,
    z_all, h_a, h_b, d_a, d_b, u_a, u_b, p_all, o_a, o_b, w_all, w_out, k_all, v_all,
    acc, low_send_a, low_recv_a, low_send_b, low_recv_b, low_parts, out_parts,
    low_mine, low_theirs, out_mine, out_theirs,
    q_rows, key_rows, value_rows, length_rows, mixed_rows,
    sib_send, sib_recv, own_sum, lists_v, slots_v, lengths_v, frequencies_v, id_columns_a, id_columns_b,
    low_a, low_b, out_low_a, out_low_b, *sums,
):
    (
        z_far, z_half, z_near, z_back, x_far, x_half, x_near, x_back, y_far, y_half, y_near, y_back,
        xu_far, xu_half, xu_near, xu_back, yu_far, yu_half, yu_near, yu_back,
        send_sem, recv_sem, local_sem,
    ) = sums
    replica = lax.axis_index("replica")
    t = lax.axis_index("tensor")
    x, y = replica // 4, replica % 4
    z, c = t // 2, t % 2
    other = 1 - c

    def wrap(v):
        return lax.rem(v + 4, 4)

    def at_x(d):
        return (wrap(x + d) * 4 + y, t)

    def at_y(d):
        return (x * 4 + wrap(y + d), t)

    def at_z(d):
        return (replica, wrap(z + d) * 2 + c)

    sibling = (replica, z * 2 + other)

    counts = {"send": 0, "local": 0}
    sent = []

    def send(src, dst, device):
        i = counts["send"]
        counts["send"] = i + 1
        copy = pltpu.make_async_remote_copy(
            src_ref=src, dst_ref=dst, send_sem=send_sem.at[i], recv_sem=recv_sem.at[i],
            device_id=device, device_id_type=MESH,
        )
        copy.start()
        sent.append(copy)
        return copy

    def local(src, dst):
        i = counts["local"]
        counts["local"] = i + 1
        copy = pltpu.make_async_copy(src, dst, local_sem.at[i])
        copy.start()
        return copy

    barrier = pltpu.get_barrier_semaphore()
    partners = [at_x(d) for d in (1, 2, 3)] + [at_y(d) for d in (1, 2, 3)]
    partners += [at_z(d) for d in (1, 2, 3)] + [sibling]
    for partner in partners:
        pl.semaphore_signal(barrier, inc=1, device_id=partner, device_id_type=MESH)

    own_small = [local(lists, lists_v), local(slots, slots_v)]
    own_h = [
        local(hidden.at[:, 0:512], h_a.at[x, 0:128]),
        local(hidden.at[:, 512:1024], h_b.at[y, 0:128]),
        local(hidden, z_all.at[t]),
    ]
    own_d = [
        local(down.at[:, :, 0:512], d_a.at[y]),
        local(down.at[:, :, 512:1024], d_b.at[x]),
    ]
    own_u = [
        local(up_q.at[:, :, 0:256], u_a.at[y, :, :, 0:256]),
        local(up_kv.at[:, 0], u_a.at[y, :, :, 256:384]),
        local(up_q.at[:, :, 256:512], u_b.at[x, :, :, 0:256]),
        local(up_kv.at[:, 1], u_b.at[x, :, :, 256:384]),
    ]
    own_p = local(down_o, p_all.at[x, y])
    own_o = [
        local(up_o.at[:, :, 0:512], o_a.at[y]),
        local(up_o.at[:, :, 512:1024], o_b.at[x]),
    ]
    own_late = [local(lengths, lengths_v), local(frequencies, frequencies_v)]

    for copy in own_small:
        copy.wait()
    wanted = lists_v[pl.ds(replica, 1), :].astype(F32).astype(BF16)
    picked = lax.broadcasted_iota(jnp.int32, (32, 128), 0) == slots_v[...]
    own_ids = mm(jnp.broadcast_to(wanted, (16, 32)), picked.astype(F32).astype(BF16))
    id_rows = jnp.concatenate([own_ids] * 4, axis=1).astype(BF16)
    for copy in own_h:
        copy.wait()
    h_a[x, 128:144, :] = id_rows
    h_b[y, 128:144, :] = id_rows
    pl.semaphore_wait(barrier, len(partners))

    arrived = set()

    def landed(copies):
        for copy in copies:
            if id(copy) not in arrived:
                arrived.add(id(copy))
                copy.wait_recv()

    def ring_rest(lo, hi, own, device):
        return [
            send(hi(own), hi(own), device(1)),
            send(lo(own), lo(own), device(-1)),
        ]

    def ring_one(lo, hi, own, device):
        return [
            send(lo(own), lo(own), device(1)),
            send(hi(own), hi(own), device(-1)),
        ] + ring_rest(lo, hi, own, device)

    def ring_two(first, lo, hi, own, device):
        before, after = wrap(own - 1), wrap(own + 1)
        landed(first[0:1])
        onward = [send(lo(before), lo(before), device(1))]
        landed(first[1:2])
        onward.append(send(hi(after), hi(after), device(-1)))
        return first + onward

    def pool_parts(pool):
        return (
            (lambda i: pool.at[i, y, 0:2], lambda i: pool.at[i, y, 2:4], x, at_x),
            (lambda i: pool.at[x, i, 4:6], lambda i: pool.at[x, i, 6:8], y, at_y),
            (lambda i: pool.at[:, i, 0:2], lambda i: pool.at[:, i, 2:4], y, at_y),
            (lambda i: pool.at[i, :, 4:6], lambda i: pool.at[i, :, 6:8], x, at_x),
        )

    def gather_one(pool):
        parts = pool_parts(pool)
        return ring_one(*parts[0]), ring_one(*parts[1])

    def gather_two(pool, a, b):
        parts = pool_parts(pool)
        return ring_two(a, *parts[0]), ring_two(b, *parts[1])

    def gather_four(pool, a, b):
        parts = pool_parts(pool)
        return ring_two(a, *parts[2]), ring_two(b, *parts[3])

    ha_parts = (lambda i: h_a.at[i, 0:80], lambda i: h_a.at[i, 80:144], x, at_x)
    hb_parts = (lambda i: h_b.at[i, 0:80], lambda i: h_b.at[i, 80:144], y, at_y)
    z_parts = (lambda i: z_all.at[i * 2 + c, 0:64], lambda i: z_all.at[i * 2 + c, 64:128], z, at_z)
    da_parts = (lambda i: d_a.at[i, 0:4], lambda i: d_a.at[i, 4:8], y, at_y)
    db_parts = (lambda i: d_b.at[i, 0:4], lambda i: d_b.at[i, 4:8], x, at_x)
    ua_parts = (lambda i: u_a.at[i, 0:4], lambda i: u_a.at[i, 4:8], y, at_y)
    ub_parts = (lambda i: u_b.at[i, 0:4], lambda i: u_b.at[i, 4:8], x, at_x)
    oa_parts = (lambda i: o_a.at[i, 0:4], lambda i: o_a.at[i, 4:8], y, at_y)
    ob_parts = (lambda i: o_b.at[i, 0:4], lambda i: o_b.at[i, 4:8], x, at_x)

    ha1 = ring_one(*ha_parts)
    hb1 = ring_one(*hb_parts)
    z1 = ring_one(*z_parts)
    s0 = send(z_all.at[t], z_all.at[t], sibling)
    for copy in own_d:
        copy.wait()
    da1 = ring_one(*da_parts)
    db1 = ring_one(*db_parts)

    w_copies = []
    for d in range(8):
        i = lax.rem(t + d, 8)
        w_copies.append(local(query_w.at[i], w_all.at[i, :, 0:512]))
        w_copies.append(local(kv_w.at[0, i], w_all.at[i, :, 512:640]))
        w_copies.append(local(kv_w.at[1, i], w_all.at[i, :, 640:768]))
    k_copy = local(keys, k_all)
    v_copy = local(values, v_all)
    o_copies = []
    for d in (2, 1, 3, 0):
        for core in (other, c):
            i = wrap(z + d) * 2 + core
            columns = pl.ds(pl.multiple_of(i * 1024, 1024), 1024)
            o_copies.append(local(out_w.at[:, columns], w_out.at[i]))

    ha2 = ring_two(ha1, *ha_parts)
    hb2 = ring_two(hb1, *hb_parts)
    z2 = ring_two(z1, *z_parts)
    landed(z1)
    up_z, down_z = wrap(z + 1), wrap(z - 1)
    s1 = send(z_all.at[up_z * 2 + c], z_all.at[up_z * 2 + c], sibling)
    s2 = send(z_all.at[down_z * 2 + c], z_all.at[down_z * 2 + c], sibling)
    da2 = ring_two(da1, *da_parts)
    db2 = ring_two(db1, *db_parts)

    for copy in w_copies:
        copy.wait()
    acc[...] = jnp.zeros_like(acc)

    def project(i):
        acc[...] += mm(z_all[i], w_all[i])

    def project_near(i, _):
        project(wrap(z + i + i // 2) * 2 + c)
        return 0

    lax.fori_loop(0, 3, project_near, 0)

    for copy in own_late:
        copy.wait()

    def column(row):
        return jnp.transpose(jnp.broadcast_to(row, (128, 128)), (1, 0))

    row_lengths = column(lengths_v[...].astype(F32))
    angles = row_lengths * frequencies_v[...]
    lane = lax.broadcasted_iota(jnp.int32, (128, 128), 1)
    cosines = jnp.cos(angles)
    sines = jnp.where(lane < 64, -jnp.sin(angles), jnp.sin(angles))
    owner_ids = column(own_ids[0:1])


    landed(z2)
    far = wrap(z + 2) * 2 + c
    s3 = send(z_all.at[far], z_all.at[far], sibling)
    landed((s0, s1, s2))

    def project_far(i, _):
        mine = wrap(z + 2) * 2 + c
        theirs = wrap(z + i + i // 2) * 2 + other
        project(jnp.where(i == 3, mine, theirs))
        return 0

    lax.fori_loop(0, 4, project_far, 0)
    landed((s3,))
    project(wrap(z + 2) * 2 + other)

    landed(ha2)
    landed(hb2)

    def ids_of(h):
        return jnp.concatenate(
            [h[i, 128:144, 0:128].astype(F32)[0:1] for i in range(4)], axis=1
        )

    def fold(h, d, ids, j, owner, total):
        rows = h[:, 0:128, :].reshape(512, 512)
        maps = d[j].reshape(384, 512)
        every = lax.dot_general(maps, rows, NT, preferred_element_type=F32)
        every = every.reshape(8, 48, 512)
        first = (owner * 8).astype(F32)
        for i in range(8):
            total = total + jnp.where(ids == first + float(i), every[i], 0.0)
        return total

    ids_a, ids_b = ids_of(h_a), ids_of(h_b)
    for i in range(4):
        id_columns_a[i] = column(ids_a[:, i * 128 : (i + 1) * 128])
        id_columns_b[i] = column(ids_b[:, i * 128 : (i + 1) * 128])
    landed(da1)
    landed(db1)
    zero_low = jnp.zeros((48, 512), F32)

    def near_a(i, total):
        j = wrap(y + i + i // 2)
        return fold(h_a, d_a, ids_a, j, x * 4 + j, total)

    def near_b(i, total):
        j = wrap(x + i + i // 2)
        return fold(h_b, d_b, ids_b, j, j * 4 + y, total)

    sum_a = lax.fori_loop(0, 3, near_a, zero_low)
    sum_b = lax.fori_loop(0, 3, near_b, zero_low)
    landed(da2)
    sum_a = fold(h_a, d_a, ids_a, wrap(y + 2), x * 4 + wrap(y + 2), sum_a)
    for i in range(4):
        low_send_a[i] = sum_a[:, i * 128 : (i + 1) * 128]
    back_a = [
        send(low_send_a.at[wrap(x + d)], low_recv_a.at[x], at_x(d)) for d in (1, 3, 2)
    ]
    landed(db2)
    sum_b = fold(h_b, d_b, ids_b, wrap(x + 2), wrap(x + 2) * 4 + y, sum_b)
    for i in range(4):
        low_send_b[i] = sum_b[:, i * 128 : (i + 1) * 128]
    back_b = [
        send(low_send_b.at[wrap(y + d)], low_recv_b.at[y], at_y(d)) for d in (1, 3, 2)
    ]

    for copy in own_u:
        copy.wait()
    ua1 = ring_one(*ua_parts)
    ub1 = ring_one(*ub_parts)
    own_p.wait()
    pa1, pb1 = gather_one(p_all)
    landed(back_a)
    landed(back_b)
    part = low_send_a[x] + low_send_b[y]
    for d in (1, 2, 3):
        part = part + low_recv_a[wrap(x + d)] + low_recv_b[wrap(y + d)]
    def over_tensor(part, mine, theirs, parts, forward):
        mine[...] = part
        landed([send(mine, theirs, sibling)])
        parts[z] = part + theirs[...]
        copies = [send(parts.at[z], parts.at[z], at_z(d)) for d in (2, 1, 3)]
        forward()
        landed(copies)
        return (parts[0] + parts[1]) + (parts[2] + parts[3])

    pools = []

    def forward_pools():
        pools.append(ring_two(ua1, *ua_parts))
        pools.append(ring_two(ub1, *ub_parts))
        pools.extend(gather_two(p_all, pa1, pb1))

    low = over_tensor(part, low_mine, low_theirs, low_parts, forward_pools)
    ua2, ub2, pa2, pb2 = pools

    def spread(low, first):
        source = lax.broadcasted_iota(jnp.int32, (128, 128), 0)
        target = lax.broadcasted_iota(jnp.int32, (128, 128), 1)
        pattern = (source == first + lax.rem(target, 16)).astype(F32).astype(BF16)
        return mm(low, pattern)

    lane_adapter = (lane // 16).astype(F32)

    def turned(low):
        padding = jnp.zeros((128 - low.shape[0], 128), F32)
        full = jnp.concatenate([low.astype(F32), padding], axis=0)
        return jnp.transpose(full, (1, 0)).astype(BF16)

    class RingSum:
        def __init__(self, far, half, near, back, device):
            self.far_block, self.half, self.near_block, self.back = far, half, near, back
            self.device = device

        def far(self, block):
            self.far_block[...] = block.astype(BF16)
            self.halves = [
                send(self.far_block.at[0:64], self.half.at[0], self.device(1)),
                send(self.far_block.at[64:128], self.half.at[1], self.device(-1)),
            ]

        def near(self, plus, minus):
            near, back = self.near_block, self.back
            self.waiting = plus[0:64], minus[64:128]
            near[0, 64:128] = plus[64:128].astype(BF16)
            near[1, 0:64] = minus[0:64].astype(BF16)
            self.blocks = [
                send(near.at[0, 64:128], back.at[0, 64:128], self.device(1)),
                send(near.at[1, 0:64], back.at[1, 0:64], self.device(-1)),
            ]

        def join(self):
            near, back = self.near_block, self.back
            landed(self.halves[0:1])
            near[0, 0:64] = (self.waiting[0] + self.half[0].astype(F32)).astype(BF16)
            self.blocks.append(send(near.at[0, 0:64], back.at[0, 0:64], self.device(1)))
            landed(self.halves[1:2])
            near[1, 64:128] = (self.waiting[1] + self.half[1].astype(F32)).astype(BF16)
            self.blocks.append(send(near.at[1, 64:128], back.at[1, 64:128], self.device(-1)))

        def total(self):
            landed(self.blocks)
            return self.back[0].astype(F32) + self.back[1].astype(F32)

    def expand(g, columns, rows, owner):
        blocks = []
        for j in range(4):
            first = (owner(j) * 8).astype(F32)
            blocks.append(jnp.where(columns[g] == lane_adapter + first, rows, 0.0).astype(BF16))
        return jnp.concatenate(blocks, axis=1)

    def owner_a(j):
        return x * 4 + j

    def owner_b(j):
        return j * 4 + y

    low_a[x] = low.astype(BF16)
    low_b[y] = low.astype(BF16)
    around_a = [send(low_a.at[x], low_a.at[x], at_x(d)) for d in (2, 1, 3)]
    around_b = [send(low_b.at[y], low_b.at[y], at_y(d)) for d in (2, 1, 3)]
    landed(pa2 + pb2)

    def early(lo, hi):
        return (
            [
                send(p_all.at[lo:hi, y, 0:2], p_all.at[lo:hi, y, 0:2], at_y(1)),
                send(p_all.at[lo:hi, y, 2:4], p_all.at[lo:hi, y, 2:4], at_y(-1)),
            ],
            [
                send(p_all.at[x, lo:hi, 4:6], p_all.at[x, lo:hi, 4:6], at_x(1)),
                send(p_all.at[x, lo:hi, 6:8], p_all.at[x, lo:hi, 6:8], at_x(-1)),
            ],
        )

    pa3, pb3 = early(0, 2)
    landed(ua2)
    landed(ub2)

    def raised(g, columns, lows, first, owner, maps):
        rows = turned(lows[g])
        for_q = expand(g, columns, spread(rows, 0), owner)
        for_kv = expand(g, columns, spread(rows, first), owner)
        return ADAPTER_SCALE * jnp.concatenate(
            [
                mm(for_q, maps[:, :, :, 0:256].reshape(512, 256)),
                mm(for_kv, maps[:, :, :, 256:384].reshape(512, 128)),
            ],
            axis=1,
        )

    def raised_a(d):
        return raised(wrap(x + d), id_columns_a, low_a, 16, owner_a, u_a)

    def raised_b(d):
        return raised(wrap(y + d), id_columns_b, low_b, 32, owner_b, u_b)

    xu = RingSum(xu_far, xu_half, xu_near, xu_back, at_x)
    yu = RingSum(yu_far, yu_half, yu_near, yu_back, at_y)
    landed(around_a[0:1])
    xu.far(raised_a(2))
    landed(around_b[0:1])
    yu.far(raised_b(2))
    more_a, more_b = early(2, 4)
    pa3, pb3 = pa3 + more_a, pb3 + more_b
    landed(around_a)
    xu.near(raised_a(1), raised_a(3))
    landed(around_b)
    yu.near(raised_b(1), raised_b(3))
    own_a, own_b = raised_a(0), raised_b(0)
    xu.join()
    yu.join()
    landed(pa3 + pb3)
    pa4, pb4 = gather_four(p_all, pa3, pb3)
    pa4, pb4 = pa4 + ring_rest(*pool_parts(p_all)[2]), pb4 + ring_rest(*pool_parts(p_all)[3])
    for copy in own_o:
        copy.wait()
    oa1 = ring_one(*oa_parts)
    ob1 = ring_one(*ob_parts)
    own_a = own_a + xu.total()
    acc[:, 0:256] += own_a[:, 0:256]
    acc[:, 512:640] += own_a[:, 256:384]
    own_b = own_b + yu.total()
    acc[:, 256:512] += own_b[:, 0:256]
    acc[:, 640:768] += own_b[:, 256:384]

    def rotated(columns):
        flat = acc[:, columns * 128 : (columns + 1) * 128]
        moved = flat * cosines + pltpu.roll(flat, 64, 1) * sines
        return moved.astype(BF16).astype(F32)

    new_key = rotated(4)
    new_value = acc[:, 640:768].astype(BF16).astype(F32)
    for i in range(8):
        rows = pl.ds(i, 128, stride=8)
        q_rows[rows, :] = rotated(i % 4)
        key_rows[rows, :] = new_key
        value_rows[rows, :] = new_value
        length_rows[rows, :] = row_lengths

    k_copy.wait()
    v_copy.wait()
    scale = 1.0 / (128.0 ** 0.5)

    def attend(b, _):
        first = pl.multiple_of(b * 256, 256)
        rows = pl.ds(first, 256)
        q = q_rows[rows, :]
        q16 = q.astype(BF16)
        scores = []
        for i in range(32):
            scores.append(
                lax.dot_general(
                    q16[i * 8 : (i + 1) * 8], k_all[b * 32 + i], NT, preferred_element_type=F32
                )
            )
        scores = jnp.concatenate(scores, axis=0) * scale
        self_score = jnp.sum(q * key_rows[rows, :], axis=1, keepdims=True) * scale
        slot = lax.broadcasted_iota(jnp.int32, (256, 128), 1).astype(F32)
        valid = slot < length_rows[rows, :]
        highest = jnp.maximum(
            jnp.max(jnp.where(valid, scores, NEGATIVE), axis=1, keepdims=True), self_score
        )
        weights = jnp.where(valid, jnp.exp(scores - highest), 0.0)
        self_weight = jnp.exp(self_score - highest)
        total = jnp.sum(weights, axis=1, keepdims=True) + self_weight
        weights16 = (weights / total).astype(BF16)
        self16 = (self_weight / total).astype(BF16).astype(F32)
        mixed = []
        for i in range(32):
            mixed.append(mm(weights16[i * 8 : (i + 1) * 8], v_all[b * 32 + i]))
        mixed_rows[rows, :] = jnp.concatenate(mixed, axis=0) + self16 * value_rows[rows, :]
        return 0

    lax.fori_loop(0, 4, attend, 0)
    oa2 = ring_two(oa1, *oa_parts)
    ob2 = ring_two(ob1, *ob_parts)
    attended = jnp.concatenate(
        [mixed_rows[pl.ds(i, 128, stride=8), :].astype(BF16) for i in range(4)], axis=1
    )

    landed(pa4 + pb4)
    own_row = own_ids[0:1]
    low_out = jnp.zeros((16, 128), F32)
    for j in range(4):
        maps = p_all[j].reshape(512, 512)
        every = lax.dot_general(maps, attended, NT, preferred_element_type=F32)
        every = every.reshape(32, 16, 128)
        for i in range(32):
            low_out = low_out + jnp.where(own_row == float(j * 32 + i), every[i], 0.0)
    out_mine[...] = low_out
    to_core = send(out_mine, out_theirs, sibling)

    for copy in o_copies:
        copy.wait()
    to_sibling = {}
    for d in (2, 1, 3, 0):
        i = wrap(z + d)
        sib_send[i] = mm(attended, w_out[i * 2 + other]).astype(BF16)
        to_sibling[d] = send(sib_send.at[i], sib_recv.at[i], sibling)

    def chip_sum(d):
        i = wrap(z + d)
        mine = mm(attended, w_out[i * 2 + c])
        landed([to_sibling[d]])
        return mine + sib_recv[i].astype(F32)

    landed([to_core])
    out_parts[z] = out_mine[...] + out_theirs[...]
    out_over_z = [send(out_parts.at[z], out_parts.at[z], at_z(d)) for d in (2, 1, 3)]
    over_z = RingSum(z_far, z_half, z_near, z_back, at_z)
    over_z.far(chip_sum(2))
    over_z.near(chip_sum(1), chip_sum(3))

    landed(out_over_z)
    low_out = (out_parts[0] + out_parts[1]) + (out_parts[2] + out_parts[3])
    out_low_a[x] = low_out.astype(BF16)
    out_low_b[y] = low_out.astype(BF16)
    around_a = [send(out_low_a.at[x], out_low_a.at[x], at_x(d)) for d in (2, 1, 3)]
    around_b = [send(out_low_b.at[y], out_low_b.at[y], at_y(d)) for d in (2, 1, 3)]
    over_z.join()

    def product(g, columns, lows, owner, maps):
        expanded = expand(g, columns, spread(turned(lows[g]), 0), owner)
        return ADAPTER_SCALE * mm(expanded, maps[...].reshape(512, 512))

    def product_a(d):
        return product(wrap(x + d), id_columns_a, out_low_a, owner_a, o_a)

    def product_b(d):
        return product(wrap(y + d), id_columns_b, out_low_b, owner_b, o_b)

    landed(oa2)
    landed(ob2)
    over_x = RingSum(x_far, x_half, x_near, x_back, at_x)
    over_y = RingSum(y_far, y_half, y_near, y_back, at_y)
    landed(around_a[0:1])
    over_x.far(product_a(2))
    landed(around_b[0:1])
    over_y.far(product_b(2))
    landed(around_a)
    over_x.near(product_a(1), product_a(3))
    landed(around_b)
    over_y.near(product_b(1), product_b(3))
    over_x.join()
    over_y.join()
    own_sum[...] = chip_sum(0)
    own_sum[:, 0:512] += product_a(0)
    own_sum[:, 512:1024] += product_b(0)
    own_sum[...] += over_z.total()
    out[:, 0:512] = own_sum[:, 0:512] + over_x.total()
    out[:, 512:1024] = own_sum[:, 512:1024] + over_y.total()

    for copy in sent:
        copy.wait_send()


def shards(
    hidden,
    query_weight,
    keyvalue_weight,
    output_weight,
    adapter_down_maps,
    adapter_up_query,
    adapter_up_keyvalue,
    adapter_down_output,
    adapter_up_output,
    cached_keys,
    cached_values,
    context_lengths,
    request_list_slots,
    group_adapter_lists,
):
    pairs = np.arange(64, dtype=np.float32) * np.float32(2.0) / np.float32(128.0)
    frequency = np.power(np.float32(ROPE_BASE), -pairs).astype(np.float32)
    frequencies = jnp.asarray(np.concatenate([frequency, frequency])[None, :])

    hbm = pl.BlockSpec(memory_space=pl.ANY)
    vmem = pl.BlockSpec(memory_space=pltpu.VMEM)
    result = pl.pallas_call(
        kernel,
        out_shape=jax.ShapeDtypeStruct((128, 1024), F32),
        in_specs=[hbm] * 15,
        out_specs=vmem,
        scratch_shapes=[
            pltpu.VMEM((8, 128, 1024), BF16),
            pltpu.VMEM((4, 144, 512), BF16),
            pltpu.VMEM((4, 144, 512), BF16),
            pltpu.VMEM((4, 8, 48, 512), BF16),
            pltpu.VMEM((4, 8, 48, 512), BF16),
            pltpu.VMEM((4, 8, 16, 384), BF16),
            pltpu.VMEM((4, 8, 16, 384), BF16),
            pltpu.VMEM((4, 4, 8, 16, 512), BF16),
            pltpu.VMEM((4, 8, 16, 512), BF16),
            pltpu.VMEM((4, 8, 16, 512), BF16),
            pltpu.VMEM((8, 1024, 768), BF16),
            pltpu.VMEM((8, 512, 1024), BF16),
            pltpu.VMEM((128, 128, 128), BF16),
            pltpu.VMEM((128, 128, 128), BF16),
            pltpu.VMEM((128, 768), F32),
            pltpu.VMEM((4, 48, 128), F32),
            pltpu.VMEM((4, 48, 128), F32),
            pltpu.VMEM((4, 48, 128), F32),
            pltpu.VMEM((4, 48, 128), F32),
            pltpu.VMEM((4, 48, 128), F32),
            pltpu.VMEM((4, 16, 128), F32),
            pltpu.VMEM((48, 128), F32),
            pltpu.VMEM((48, 128), F32),
            pltpu.VMEM((16, 128), F32),
            pltpu.VMEM((16, 128), F32),
            pltpu.VMEM((1024, 128), F32),
            pltpu.VMEM((1024, 128), F32),
            pltpu.VMEM((1024, 128), F32),
            pltpu.VMEM((1024, 128), F32),
            pltpu.VMEM((1024, 128), F32),
            pltpu.VMEM((4, 128, 1024), BF16),
            pltpu.VMEM((4, 128, 1024), BF16),
            pltpu.VMEM((128, 1024), F32),
            pltpu.VMEM((16, 32), jnp.int32),
            pltpu.VMEM((1, 128), jnp.int32),
            pltpu.VMEM((1, 128), jnp.int32),
            pltpu.VMEM((1, 128), F32),
            pltpu.VMEM((4, 128, 128), F32),
            pltpu.VMEM((4, 128, 128), F32),
            pltpu.VMEM((4, 48, 128), BF16),
            pltpu.VMEM((4, 48, 128), BF16),
            pltpu.VMEM((4, 16, 128), BF16),
            pltpu.VMEM((4, 16, 128), BF16),
            pltpu.VMEM((128, 1024), BF16),
            pltpu.VMEM((2, 64, 1024), BF16),
            pltpu.VMEM((2, 128, 1024), BF16),
            pltpu.VMEM((2, 128, 1024), BF16),
            pltpu.VMEM((128, 512), BF16),
            pltpu.VMEM((2, 64, 512), BF16),
            pltpu.VMEM((2, 128, 512), BF16),
            pltpu.VMEM((2, 128, 512), BF16),
            pltpu.VMEM((128, 512), BF16),
            pltpu.VMEM((2, 64, 512), BF16),
            pltpu.VMEM((2, 128, 512), BF16),
            pltpu.VMEM((2, 128, 512), BF16),
            pltpu.VMEM((128, 384), BF16),
            pltpu.VMEM((2, 64, 384), BF16),
            pltpu.VMEM((2, 128, 384), BF16),
            pltpu.VMEM((2, 128, 384), BF16),
            pltpu.VMEM((128, 384), BF16),
            pltpu.VMEM((2, 64, 384), BF16),
            pltpu.VMEM((2, 128, 384), BF16),
            pltpu.VMEM((2, 128, 384), BF16),
            pltpu.SemaphoreType.DMA((SENDS,)),
            pltpu.SemaphoreType.DMA((SENDS,)),
            pltpu.SemaphoreType.DMA((LOCALS,)),
        ],
        compiler_params=pltpu.CompilerParams(
            collective_id=0, has_side_effects=True, vmem_limit_bytes=62 * 1024 * 1024
        ),
        cost_estimate=pl.CostEstimate(flops=8_000_000_000, bytes_accessed=32_000_000, transcendentals=0),
    )(
        hidden,
        group_adapter_lists,
        request_list_slots[None, :],
        context_lengths[None, :],
        frequencies,
        query_weight.reshape(8, 1024, 512),
        keyvalue_weight.reshape(2, 8, 1024, 128),
        output_weight,
        jnp.transpose(adapter_down_maps, (0, 2, 1)),
        adapter_up_query,
        adapter_up_keyvalue,
        jnp.transpose(adapter_down_output, (0, 2, 1)),
        adapter_up_output,
        cached_keys.reshape(128, 128, 128),
        cached_values.reshape(128, 128, 128),
    )
    return result.astype(BF16)


def solution(mesh):
    in_specs = (
        P("replica", "tensor"),
        P(None, "tensor"),
        P(None, None, "tensor"),
        P("tensor", None),
        P("replica", "tensor", None),
        P("replica", None, "tensor"),
        P("replica", None, None, "tensor"),
        P("replica", "tensor", None),
        P("replica", None, "tensor"),
        P("replica", "tensor", None, None),
        P("replica", "tensor", None, None),
        P("replica"),
        P("replica"),
        P(),
    )
    out_specs = P("replica", "tensor")
    return jax.shard_map(shards, mesh=mesh, in_specs=in_specs, out_specs=out_specs, check_vma=False)
```

```python
import functools

import jax
import jax.numpy as jnp
import numpy as np
from jax import lax
from jax.experimental import pallas as pl
from jax.experimental.pallas import tpu as pltpu
from jax.sharding import PartitionSpec as P

ADAPTER_SCALE = 2.0
ROPE_BASE = 500000.0
MESH = pl.DeviceIdType.MESH
BF16 = jnp.bfloat16
F32 = jnp.float32
NT = (((1,), (1,)), ((), ()))
NEGATIVE = -1e30
SENDS = 160
LOCALS = 64


def mm(a, b):
    return jnp.dot(a, b, preferred_element_type=F32)


def kernel(
    hidden, lists, slots, lengths, frequencies,
    query_w, kv_w, out_w, down, up_q, up_kv, down_o, up_o, keys, values,
    out,
    z_all, h_a, h_b, d_a, d_b, u_a, u_b, p_all, o_a, o_b, w_all, w_out, k_all, v_all,
    acc, low_send_a, low_recv_a, low_send_b, low_recv_b, low_parts, out_parts,
    low_mine, low_theirs, out_mine, out_theirs,
    q_rows, key_rows, value_rows, length_rows, mixed_rows,
    sib_send, sib_recv, own_sum, lists_v, slots_v, lengths_v, frequencies_v, id_columns_a, id_columns_b,
    low_a, low_b, out_low_a, out_low_b, *sums,
):
    (
        z_far, z_half, z_near, z_back, x_far, x_half, x_near, x_back, y_far, y_half, y_near, y_back,
        xu_far, xu_half, xu_near, xu_back, yu_far, yu_half, yu_near, yu_back,
        send_sem, recv_sem, local_sem,
    ) = sums
    replica = lax.axis_index("replica")
    t = lax.axis_index("tensor")
    x, y = replica // 4, replica % 4
    z, c = t // 2, t % 2
    other = 1 - c

    def wrap(v):
        return lax.rem(v + 4, 4)

    def at_x(d):
        return (wrap(x + d) * 4 + y, t)

    def at_y(d):
        return (x * 4 + wrap(y + d), t)

    def at_z(d):
        return (replica, wrap(z + d) * 2 + c)

    sibling = (replica, z * 2 + other)

    counts = {"send": 0, "local": 0}
    sent = []

    def send(src, dst, device):
        i = counts["send"]
        counts["send"] = i + 1
        copy = pltpu.make_async_remote_copy(
            src_ref=src, dst_ref=dst, send_sem=send_sem.at[i], recv_sem=recv_sem.at[i],
            device_id=device, device_id_type=MESH,
        )
        copy.start()
        sent.append(copy)
        return copy

    def local(src, dst):
        i = counts["local"]
        counts["local"] = i + 1
        copy = pltpu.make_async_copy(src, dst, local_sem.at[i])
        copy.start()
        return copy

    barrier = pltpu.get_barrier_semaphore()
    partners = [at_x(d) for d in (1, 2, 3)] + [at_y(d) for d in (1, 2, 3)]
    partners += [at_z(d) for d in (1, 2, 3)] + [sibling]
    for partner in partners:
        pl.semaphore_signal(barrier, inc=1, device_id=partner, device_id_type=MESH)

    own_small = [local(lists, lists_v), local(slots, slots_v)]
    own_h = [
        local(hidden.at[:, 0:512], h_a.at[x, 0:128]),
        local(hidden.at[:, 512:1024], h_b.at[y, 0:128]),
        local(hidden, z_all.at[t]),
    ]
    own_d = [
        local(down.at[:, :, 0:512], d_a.at[y]),
        local(down.at[:, :, 512:1024], d_b.at[x]),
    ]
    own_u = [
        local(up_q.at[:, :, 0:256], u_a.at[y, :, :, 0:256]),
        local(up_kv.at[:, 0], u_a.at[y, :, :, 256:384]),
        local(up_q.at[:, :, 256:512], u_b.at[x, :, :, 0:256]),
        local(up_kv.at[:, 1], u_b.at[x, :, :, 256:384]),
    ]
    own_p = local(down_o, p_all.at[x, y])
    own_o = [
        local(up_o.at[:, :, 0:512], o_a.at[y]),
        local(up_o.at[:, :, 512:1024], o_b.at[x]),
    ]
    own_late = [local(lengths, lengths_v), local(frequencies, frequencies_v)]

    for copy in own_small:
        copy.wait()
    wanted = lists_v[pl.ds(replica, 1), :].astype(F32).astype(BF16)
    picked = lax.broadcasted_iota(jnp.int32, (32, 128), 0) == slots_v[...]
    own_ids = mm(jnp.broadcast_to(wanted, (16, 32)), picked.astype(F32).astype(BF16))
    id_rows = jnp.concatenate([own_ids] * 4, axis=1).astype(BF16)
    for copy in own_h:
        copy.wait()
    h_a[x, 128:144, :] = id_rows
    h_b[y, 128:144, :] = id_rows
    pl.semaphore_wait(barrier, len(partners))

    arrived = set()

    def landed(copies):
        for copy in copies:
            if id(copy) not in arrived:
                arrived.add(id(copy))
                copy.wait_recv()

    def ring_rest(lo, hi, own, device):
        return [
            send(hi(own), hi(own), device(1)),
            send(lo(own), lo(own), device(-1)),
        ]

    def ring_one(lo, hi, own, device):
        return [
            send(lo(own), lo(own), device(1)),
            send(hi(own), hi(own), device(-1)),
        ] + ring_rest(lo, hi, own, device)

    def ring_two(first, lo, hi, own, device):
        before, after = wrap(own - 1), wrap(own + 1)
        landed(first[0:1])
        onward = [send(lo(before), lo(before), device(1))]
        landed(first[1:2])
        onward.append(send(hi(after), hi(after), device(-1)))
        return first + onward

    def pool_parts(pool):
        return (
            (lambda i: pool.at[i, y, 0:2], lambda i: pool.at[i, y, 2:4], x, at_x),
            (lambda i: pool.at[x, i, 4:6], lambda i: pool.at[x, i, 6:8], y, at_y),
            (lambda i: pool.at[:, i, 0:2], lambda i: pool.at[:, i, 2:4], y, at_y),
            (lambda i: pool.at[i, :, 4:6], lambda i: pool.at[i, :, 6:8], x, at_x),
        )

    def gather_one(pool):
        parts = pool_parts(pool)
        return ring_one(*parts[0]), ring_one(*parts[1])

    def gather_two(pool, a, b):
        parts = pool_parts(pool)
        return ring_two(a, *parts[0]), ring_two(b, *parts[1])

    def gather_four(pool, a, b):
        parts = pool_parts(pool)
        return ring_two(a, *parts[2]), ring_two(b, *parts[3])

    ha_parts = (lambda i: h_a.at[i, 0:80], lambda i: h_a.at[i, 80:144], x, at_x)
    hb_parts = (lambda i: h_b.at[i, 0:80], lambda i: h_b.at[i, 80:144], y, at_y)
    z_parts = (lambda i: z_all.at[i * 2 + c, 0:64], lambda i: z_all.at[i * 2 + c, 64:128], z, at_z)
    da_parts = (lambda i: d_a.at[i, 0:4], lambda i: d_a.at[i, 4:8], y, at_y)
    db_parts = (lambda i: d_b.at[i, 0:4], lambda i: d_b.at[i, 4:8], x, at_x)
    ua_parts = (lambda i: u_a.at[i, 0:4], lambda i: u_a.at[i, 4:8], y, at_y)
    ub_parts = (lambda i: u_b.at[i, 0:4], lambda i: u_b.at[i, 4:8], x, at_x)
    oa_parts = (lambda i: o_a.at[i, 0:4], lambda i: o_a.at[i, 4:8], y, at_y)
    ob_parts = (lambda i: o_b.at[i, 0:4], lambda i: o_b.at[i, 4:8], x, at_x)

    ha1 = ring_one(*ha_parts)
    hb1 = ring_one(*hb_parts)
    z1 = ring_one(*z_parts)
    s0 = send(z_all.at[t], z_all.at[t], sibling)
    for copy in own_d:
        copy.wait()
    da1 = ring_one(*da_parts)
    db1 = ring_one(*db_parts)

    w_copies = []
    for d in range(8):
        i = lax.rem(t + d, 8)
        w_copies.append(local(query_w.at[i], w_all.at[i, :, 0:512]))
        w_copies.append(local(kv_w.at[0, i], w_all.at[i, :, 512:640]))
        w_copies.append(local(kv_w.at[1, i], w_all.at[i, :, 640:768]))
    k_copy = local(keys, k_all)
    v_copy = local(values, v_all)
    o_copies = []
    for d in (2, 1, 3, 0):
        for core in (other, c):
            i = wrap(z + d) * 2 + core
            columns = pl.ds(pl.multiple_of(i * 1024, 1024), 1024)
            o_copies.append(local(out_w.at[:, columns], w_out.at[i]))

    ha2 = ring_two(ha1, *ha_parts)
    hb2 = ring_two(hb1, *hb_parts)
    z2 = ring_two(z1, *z_parts)
    landed(z1)
    up_z, down_z = wrap(z + 1), wrap(z - 1)
    s1 = send(z_all.at[up_z * 2 + c], z_all.at[up_z * 2 + c], sibling)
    s2 = send(z_all.at[down_z * 2 + c], z_all.at[down_z * 2 + c], sibling)
    da2 = ring_two(da1, *da_parts)
    db2 = ring_two(db1, *db_parts)

    for copy in w_copies:
        copy.wait()
    acc[...] = jnp.zeros_like(acc)

    def project(i):
        acc[...] += mm(z_all[i], w_all[i])

    def project_near(i, _):
        project(wrap(z + i + i // 2) * 2 + c)
        return 0

    lax.fori_loop(0, 3, project_near, 0)

    for copy in own_late:
        copy.wait()

    def column(row):
        return jnp.transpose(jnp.broadcast_to(row, (128, 128)), (1, 0))

    row_lengths = column(lengths_v[...].astype(F32))
    angles = row_lengths * frequencies_v[...]
    lane = lax.broadcasted_iota(jnp.int32, (128, 128), 1)
    cosines = jnp.cos(angles)
    sines = jnp.where(lane < 64, -jnp.sin(angles), jnp.sin(angles))
    for i in range(8):
        length_rows[pl.ds(i, 128, stride=8), :] = row_lengths


    landed(z2)
    far = wrap(z + 2) * 2 + c
    s3 = send(z_all.at[far], z_all.at[far], sibling)
    landed((s0, s1, s2))

    def project_far(i, _):
        mine = wrap(z + 2) * 2 + c
        theirs = wrap(z + i + i // 2) * 2 + other
        project(jnp.where(i == 3, mine, theirs))
        return 0

    lax.fori_loop(0, 4, project_far, 0)
    landed((s3,))
    project(wrap(z + 2) * 2 + other)

    landed(ha2)
    landed(hb2)

    def ids_of(h):
        return jnp.concatenate(
            [h[i, 128:144, 0:128].astype(F32)[0:1] for i in range(4)], axis=1
        )

    def fold(h, d, ids, j, owner, total):
        rows = h[:, 0:128, :].reshape(512, 512)
        maps = d[j].reshape(384, 512)
        every = lax.dot_general(maps, rows, NT, preferred_element_type=F32)
        every = every.reshape(8, 48, 512)
        first = (owner * 8).astype(F32)
        for i in range(8):
            total = total + jnp.where(ids == first + float(i), every[i], 0.0)
        return total

    ids_a, ids_b = ids_of(h_a), ids_of(h_b)
    for i in range(4):
        id_columns_a[i] = column(ids_a[:, i * 128 : (i + 1) * 128])
        id_columns_b[i] = column(ids_b[:, i * 128 : (i + 1) * 128])
    landed(da1)
    landed(db1)
    zero_low = jnp.zeros((48, 512), F32)

    def near_a(i, total):
        j = wrap(y + i + i // 2)
        return fold(h_a, d_a, ids_a, j, x * 4 + j, total)

    def near_b(i, total):
        j = wrap(x + i + i // 2)
        return fold(h_b, d_b, ids_b, j, j * 4 + y, total)

    sum_a = lax.fori_loop(0, 3, near_a, zero_low)
    sum_b = lax.fori_loop(0, 3, near_b, zero_low)
    landed(da2)
    sum_a = fold(h_a, d_a, ids_a, wrap(y + 2), x * 4 + wrap(y + 2), sum_a)
    for i in range(4):
        low_send_a[i] = sum_a[:, i * 128 : (i + 1) * 128]
    back_a = [
        send(low_send_a.at[wrap(x + d)], low_recv_a.at[x], at_x(d)) for d in (1, 3, 2)
    ]
    landed(db2)
    sum_b = fold(h_b, d_b, ids_b, wrap(x + 2), wrap(x + 2) * 4 + y, sum_b)
    for i in range(4):
        low_send_b[i] = sum_b[:, i * 128 : (i + 1) * 128]
    back_b = [
        send(low_send_b.at[wrap(y + d)], low_recv_b.at[y], at_y(d)) for d in (1, 3, 2)
    ]

    own_p.wait()
    pa1, pb1 = gather_one(p_all)
    for copy in own_u:
        copy.wait()
    ua1 = ring_one(*ua_parts)
    ub1 = ring_one(*ub_parts)
    landed(back_a)
    landed(back_b)
    part = low_send_a[x] + low_send_b[y]
    for d in (1, 2, 3):
        part = part + low_recv_a[wrap(x + d)] + low_recv_b[wrap(y + d)]
    def over_tensor(part, mine, theirs, parts, forward_first, forward):
        mine[...] = part
        to_core = send(mine, theirs, sibling)
        forward_first()
        landed([to_core])
        parts[z] = part + theirs[...]
        copies = [send(parts.at[z], parts.at[z], at_z(d)) for d in (2, 1, 3)]
        forward()
        landed(copies)
        return (parts[0] + parts[1]) + (parts[2] + parts[3])

    def piece(lo, hi, first, second):
        return (
            [
                send(p_all.at[lo:hi, y, first : first + 2], p_all.at[lo:hi, y, first : first + 2], at_y(1)),
                send(p_all.at[lo:hi, y, second : second + 2], p_all.at[lo:hi, y, second : second + 2], at_y(-1)),
            ],
            [
                send(p_all.at[x, lo:hi, first + 4 : first + 6], p_all.at[x, lo:hi, first + 4 : first + 6], at_x(1)),
                send(p_all.at[x, lo:hi, second + 4 : second + 6], p_all.at[x, lo:hi, second + 4 : second + 6], at_x(-1)),
            ],
        )

    pools = []

    def forward_p():
        pools.extend(gather_two(p_all, pa1, pb1))

    def forward_u():
        pools.append(ring_two(ua1, *ua_parts))
        pools.append(ring_two(ub1, *ub_parts))
        landed(pools[0] + pools[1])
        pools.extend(piece(0, 2, 0, 2))

    low = over_tensor(part, low_mine, low_theirs, low_parts, forward_p, forward_u)
    pa2, pb2, ua2, ub2, pa3, pb3 = pools

    def spread(low, first):
        source = lax.broadcasted_iota(jnp.int32, (128, 128), 0)
        target = lax.broadcasted_iota(jnp.int32, (128, 128), 1)
        pattern = (source == first + lax.rem(target, 16)).astype(F32).astype(BF16)
        return mm(low, pattern)

    lane_adapter = (lane // 16).astype(F32)

    def turned(low):
        padding = jnp.zeros((128 - low.shape[0], 128), F32)
        full = jnp.concatenate([low.astype(F32), padding], axis=0)
        return jnp.transpose(full, (1, 0)).astype(BF16)

    class RingSum:
        def __init__(self, far, half, near, back, device):
            self.far_block, self.half, self.near_block, self.back = far, half, near, back
            self.device = device

        def far(self, block):
            self.far_block[...] = block.astype(BF16)
            self.halves = [
                send(self.far_block.at[0:64], self.half.at[0], self.device(1)),
                send(self.far_block.at[64:128], self.half.at[1], self.device(-1)),
            ]

        def near(self, plus, minus):
            near, back = self.near_block, self.back
            self.waiting = plus[0:64], minus[64:128]
            near[0, 64:128] = plus[64:128].astype(BF16)
            near[1, 0:64] = minus[0:64].astype(BF16)
            self.blocks = [
                send(near.at[0, 64:128], back.at[0, 64:128], self.device(1)),
                send(near.at[1, 0:64], back.at[1, 0:64], self.device(-1)),
            ]

        def join(self):
            near, back = self.near_block, self.back
            landed(self.halves[0:1])
            near[0, 0:64] = (self.waiting[0] + self.half[0].astype(F32)).astype(BF16)
            self.blocks.append(send(near.at[0, 0:64], back.at[0, 0:64], self.device(1)))
            landed(self.halves[1:2])
            near[1, 64:128] = (self.waiting[1] + self.half[1].astype(F32)).astype(BF16)
            self.blocks.append(send(near.at[1, 64:128], back.at[1, 64:128], self.device(-1)))

        def total(self):
            landed(self.blocks)
            return self.back[0].astype(F32) + self.back[1].astype(F32)

    def expand(g, columns, rows, owner):
        blocks = []
        for j in range(4):
            first = (owner(j) * 8).astype(F32)
            blocks.append(jnp.where(columns[g] == lane_adapter + first, rows, 0.0).astype(BF16))
        return jnp.concatenate(blocks, axis=1)

    def owner_a(j):
        return x * 4 + j

    def owner_b(j):
        return j * 4 + y

    low_a[x] = low.astype(BF16)
    low_b[y] = low.astype(BF16)
    around_a = [send(low_a.at[x], low_a.at[x], at_x(d)) for d in (2, 1, 3)]
    around_b = [send(low_b.at[y], low_b.at[y], at_y(d)) for d in (2, 1, 3)]
    more_a, more_b = piece(2, 4, 0, 2)
    pa3, pb3 = pa3 + more_a, pb3 + more_b
    landed(ua2)
    landed(ub2)

    def raised(g, columns, lows, first, owner, maps):
        rows = turned(lows[g])
        for_q = expand(g, columns, spread(rows, 0), owner)
        for_kv = expand(g, columns, spread(rows, first), owner)
        return ADAPTER_SCALE * jnp.concatenate(
            [
                mm(for_q, maps[:, :, :, 0:256].reshape(512, 256)),
                mm(for_kv, maps[:, :, :, 256:384].reshape(512, 128)),
            ],
            axis=1,
        )

    def raised_a(d):
        return raised(wrap(x + d), id_columns_a, low_a, 16, owner_a, u_a)

    def raised_b(d):
        return raised(wrap(y + d), id_columns_b, low_b, 32, owner_b, u_b)

    xu = RingSum(xu_far, xu_half, xu_near, xu_back, at_x)
    yu = RingSum(yu_far, yu_half, yu_near, yu_back, at_y)
    landed(around_a[0:1])
    xu.far(raised_a(2))
    landed(around_b[0:1])
    yu.far(raised_b(2))
    rest_a, rest_b = piece(0, 2, 2, 0)
    landed(around_a)
    xu.near(raised_a(1), raised_a(3))
    landed(around_b)
    yu.near(raised_b(1), raised_b(3))
    own_a, own_b = raised_a(0), raised_b(0)
    xu.join()
    yu.join()
    landed(pa3 + pb3)
    pa4, pb4 = gather_four(p_all, pa3, pb3)
    more_a, more_b = piece(2, 4, 2, 0)
    pa4, pb4 = pa4 + rest_a + more_a, pb4 + rest_b + more_b
    for copy in own_o:
        copy.wait()
    oa1 = ring_one(*oa_parts)
    ob1 = ring_one(*ob_parts)
    own_a = own_a + xu.total()
    acc[:, 0:256] += own_a[:, 0:256]
    acc[:, 512:640] += own_a[:, 256:384]
    own_b = own_b + yu.total()
    acc[:, 256:512] += own_b[:, 0:256]
    acc[:, 640:768] += own_b[:, 256:384]

    def rotated(columns):
        flat = acc[:, columns * 128 : (columns + 1) * 128]
        moved = flat * cosines + pltpu.roll(flat, 64, 1) * sines
        return moved.astype(BF16).astype(F32)

    new_key = rotated(4)
    new_value = acc[:, 640:768].astype(BF16).astype(F32)
    for i in range(8):
        rows = pl.ds(i, 128, stride=8)
        q_rows[rows, :] = rotated(i % 4)
        key_rows[rows, :] = new_key
        value_rows[rows, :] = new_value

    k_copy.wait()
    v_copy.wait()
    scale = 1.0 / (128.0 ** 0.5)

    def attend(b, _):
        first = pl.multiple_of(b * 256, 256)
        rows = pl.ds(first, 256)
        q = q_rows[rows, :]
        q16 = q.astype(BF16)
        scores = []
        for i in range(16):
            pair = k_all[pl.ds(b * 32 + 2 * i, 2)].reshape(256, 128)
            both = lax.dot_general(
                q16[i * 16 : (i + 1) * 16], pair, NT, preferred_element_type=F32
            )
            scores.append(both[0:8, 0:128])
            scores.append(both[8:16, 128:256])
        scores = jnp.concatenate(scores, axis=0) * scale
        self_score = jnp.sum(q * key_rows[rows, :], axis=1, keepdims=True) * scale
        slot = lax.broadcasted_iota(jnp.int32, (256, 128), 1).astype(F32)
        valid = slot < length_rows[rows, :]
        highest = jnp.maximum(
            jnp.max(jnp.where(valid, scores, NEGATIVE), axis=1, keepdims=True), self_score
        )
        weights = jnp.where(valid, jnp.exp(scores - highest), 0.0)
        self_weight = jnp.exp(self_score - highest)
        total = jnp.sum(weights, axis=1, keepdims=True) + self_weight
        weights = weights / total
        even = lax.rem(lax.broadcasted_iota(jnp.int32, (256, 128), 0), 16) < 8
        weights16 = jnp.concatenate(
            [jnp.where(even, weights, 0.0), jnp.where(even, 0.0, weights)], axis=1
        ).astype(BF16)
        self16 = (self_weight / total).astype(BF16).astype(F32)
        mixed = []
        for i in range(16):
            pair = v_all[pl.ds(b * 32 + 2 * i, 2)].reshape(256, 128)
            mixed.append(mm(weights16[i * 16 : (i + 1) * 16], pair))
        mixed_rows[rows, :] = jnp.concatenate(mixed, axis=0) + self16 * value_rows[rows, :]
        return 0

    lax.fori_loop(0, 4, attend, 0)
    attended = jnp.concatenate(
        [mixed_rows[pl.ds(i, 128, stride=8), :].astype(BF16) for i in range(4)], axis=1
    )

    before_output = len(sent)

    for copy in o_copies:
        copy.wait()
    to_sibling = {}
    for d in (2, 1, 3, 0):
        i = wrap(z + d)
        sib_send[i] = mm(attended, w_out[i * 2 + other]).astype(BF16)
        to_sibling[d] = send(sib_send.at[i], sib_recv.at[i], sibling)

    landed(pa4 + pb4)
    own_row = own_ids[0:1]
    low_out = jnp.zeros((16, 128), F32)
    for j in range(4):
        maps = p_all[j].reshape(512, 512)
        every = lax.dot_general(maps, attended, NT, preferred_element_type=F32)
        every = every.reshape(32, 16, 128)
        for i in range(32):
            low_out = low_out + jnp.where(own_row == float(j * 32 + i), every[i], 0.0)
    out_mine[...] = low_out
    to_core = send(out_mine, out_theirs, sibling)

    def chip_sum(d):
        i = wrap(z + d)
        mine = mm(attended, w_out[i * 2 + c])
        landed([to_sibling[d]])
        return mine + sib_recv[i].astype(F32)

    oa2 = ring_two(oa1, *oa_parts)
    ob2 = ring_two(ob1, *ob_parts)
    landed([to_core])
    out_parts[z] = out_mine[...] + out_theirs[...]
    out_over_z = [send(out_parts.at[z], out_parts.at[z], at_z(d)) for d in (2, 1, 3)]
    over_z = RingSum(z_far, z_half, z_near, z_back, at_z)
    over_z.far(chip_sum(2))
    over_z.near(chip_sum(1), chip_sum(3))

    landed(out_over_z)
    low_out = (out_parts[0] + out_parts[1]) + (out_parts[2] + out_parts[3])
    out_low_a[x] = low_out.astype(BF16)
    out_low_b[y] = low_out.astype(BF16)
    around_a = [send(out_low_a.at[x], out_low_a.at[x], at_x(d)) for d in (2, 1, 3)]
    around_b = [send(out_low_b.at[y], out_low_b.at[y], at_y(d)) for d in (2, 1, 3)]
    for copy in sent[:before_output]:
        copy.wait_send()
    over_z.join()

    def product(g, columns, lows, owner, maps):
        expanded = expand(g, columns, spread(turned(lows[g]), 0), owner)
        return ADAPTER_SCALE * mm(expanded, maps[...].reshape(512, 512))

    def product_a(d):
        return product(wrap(x + d), id_columns_a, out_low_a, owner_a, o_a)

    def product_b(d):
        return product(wrap(y + d), id_columns_b, out_low_b, owner_b, o_b)

    landed(oa2)
    landed(ob2)
    over_x = RingSum(x_far, x_half, x_near, x_back, at_x)
    over_y = RingSum(y_far, y_half, y_near, y_back, at_y)
    landed(around_a[0:1])
    over_x.far(product_a(2))
    landed(around_b[0:1])
    over_y.far(product_b(2))
    landed(around_a)
    over_x.near(product_a(1), product_a(3))
    landed(around_b)
    over_y.near(product_b(1), product_b(3))
    over_x.join()
    over_y.join()
    own_sum[...] = chip_sum(0)
    own_sum[:, 0:512] += product_a(0)
    own_sum[:, 512:1024] += product_b(0)
    own_sum[...] += over_z.total()
    out[:, 0:512] = own_sum[:, 0:512] + over_x.total()
    out[:, 512:1024] = own_sum[:, 512:1024] + over_y.total()

    for copy in sent[before_output:]:
        copy.wait_send()


def shards(
    hidden,
    query_weight,
    keyvalue_weight,
    output_weight,
    adapter_down_maps,
    adapter_up_query,
    adapter_up_keyvalue,
    adapter_down_output,
    adapter_up_output,
    cached_keys,
    cached_values,
    context_lengths,
    request_list_slots,
    group_adapter_lists,
):
    pairs = np.arange(64, dtype=np.float32) * np.float32(2.0) / np.float32(128.0)
    frequency = np.power(np.float32(ROPE_BASE), -pairs).astype(np.float32)
    frequencies = jnp.asarray(np.concatenate([frequency, frequency])[None, :])

    hbm = pl.BlockSpec(memory_space=pl.ANY)
    vmem = pl.BlockSpec(memory_space=pltpu.VMEM)
    result = pl.pallas_call(
        kernel,
        out_shape=jax.ShapeDtypeStruct((128, 1024), F32),
        in_specs=[hbm] * 15,
        out_specs=vmem,
        scratch_shapes=[
            pltpu.VMEM((8, 128, 1024), BF16),
            pltpu.VMEM((4, 144, 512), BF16),
            pltpu.VMEM((4, 144, 512), BF16),
            pltpu.VMEM((4, 8, 48, 512), BF16),
            pltpu.VMEM((4, 8, 48, 512), BF16),
            pltpu.VMEM((4, 8, 16, 384), BF16),
            pltpu.VMEM((4, 8, 16, 384), BF16),
            pltpu.VMEM((4, 4, 8, 16, 512), BF16),
            pltpu.VMEM((4, 8, 16, 512), BF16),
            pltpu.VMEM((4, 8, 16, 512), BF16),
            pltpu.VMEM((8, 1024, 768), BF16),
            pltpu.VMEM((8, 512, 1024), BF16),
            pltpu.VMEM((128, 128, 128), BF16),
            pltpu.VMEM((128, 128, 128), BF16),
            pltpu.VMEM((128, 768), F32),
            pltpu.VMEM((4, 48, 128), F32),
            pltpu.VMEM((4, 48, 128), F32),
            pltpu.VMEM((4, 48, 128), F32),
            pltpu.VMEM((4, 48, 128), F32),
            pltpu.VMEM((4, 48, 128), F32),
            pltpu.VMEM((4, 16, 128), F32),
            pltpu.VMEM((48, 128), F32),
            pltpu.VMEM((48, 128), F32),
            pltpu.VMEM((16, 128), F32),
            pltpu.VMEM((16, 128), F32),
            pltpu.VMEM((1024, 128), F32),
            pltpu.VMEM((1024, 128), F32),
            pltpu.VMEM((1024, 128), F32),
            pltpu.VMEM((1024, 128), F32),
            pltpu.VMEM((1024, 128), F32),
            pltpu.VMEM((4, 128, 1024), BF16),
            pltpu.VMEM((4, 128, 1024), BF16),
            pltpu.VMEM((128, 1024), F32),
            pltpu.VMEM((16, 32), jnp.int32),
            pltpu.VMEM((1, 128), jnp.int32),
            pltpu.VMEM((1, 128), jnp.int32),
            pltpu.VMEM((1, 128), F32),
            pltpu.VMEM((4, 128, 128), F32),
            pltpu.VMEM((4, 128, 128), F32),
            pltpu.VMEM((4, 48, 128), BF16),
            pltpu.VMEM((4, 48, 128), BF16),
            pltpu.VMEM((4, 16, 128), BF16),
            pltpu.VMEM((4, 16, 128), BF16),
            pltpu.VMEM((128, 1024), BF16),
            pltpu.VMEM((2, 64, 1024), BF16),
            pltpu.VMEM((2, 128, 1024), BF16),
            pltpu.VMEM((2, 128, 1024), BF16),
            pltpu.VMEM((128, 512), BF16),
            pltpu.VMEM((2, 64, 512), BF16),
            pltpu.VMEM((2, 128, 512), BF16),
            pltpu.VMEM((2, 128, 512), BF16),
            pltpu.VMEM((128, 512), BF16),
            pltpu.VMEM((2, 64, 512), BF16),
            pltpu.VMEM((2, 128, 512), BF16),
            pltpu.VMEM((2, 128, 512), BF16),
            pltpu.VMEM((128, 384), BF16),
            pltpu.VMEM((2, 64, 384), BF16),
            pltpu.VMEM((2, 128, 384), BF16),
            pltpu.VMEM((2, 128, 384), BF16),
            pltpu.VMEM((128, 384), BF16),
            pltpu.VMEM((2, 64, 384), BF16),
            pltpu.VMEM((2, 128, 384), BF16),
            pltpu.VMEM((2, 128, 384), BF16),
            pltpu.SemaphoreType.DMA((SENDS,)),
            pltpu.SemaphoreType.DMA((SENDS,)),
            pltpu.SemaphoreType.DMA((LOCALS,)),
        ],
        compiler_params=pltpu.CompilerParams(
            collective_id=0, has_side_effects=True, vmem_limit_bytes=62 * 1024 * 1024
        ),
        cost_estimate=pl.CostEstimate(flops=8_000_000_000, bytes_accessed=32_000_000, transcendentals=0),
    )(
        hidden,
        group_adapter_lists,
        request_list_slots[None, :],
        context_lengths[None, :],
        frequencies,
        query_weight.reshape(8, 1024, 512),
        keyvalue_weight.reshape(2, 8, 1024, 128),
        output_weight,
        jnp.transpose(adapter_down_maps, (0, 2, 1)),
        adapter_up_query,
        adapter_up_keyvalue,
        jnp.transpose(adapter_down_output, (0, 2, 1)),
        adapter_up_output,
        cached_keys.reshape(128, 128, 128),
        cached_values.reshape(128, 128, 128),
    )
    return result.astype(BF16)


def solution(mesh):
    in_specs = (
        P("replica", "tensor"),
        P(None, "tensor"),
        P(None, None, "tensor"),
        P("tensor", None),
        P("replica", "tensor", None),
        P("replica", None, "tensor"),
        P("replica", None, None, "tensor"),
        P("replica", "tensor", None),
        P("replica", None, "tensor"),
        P("replica", "tensor", None, None),
        P("replica", "tensor", None, None),
        P("replica"),
        P("replica"),
        P(),
    )
    out_specs = P("replica", "tensor")
    return jax.shard_map(shards, mesh=mesh, in_specs=in_specs, out_specs=out_specs, check_vma=False)
```

```python
import functools

import jax
import jax.numpy as jnp
import numpy as np
from jax import lax
from jax.experimental import pallas as pl
from jax.experimental.pallas import tpu as pltpu
from jax.sharding import PartitionSpec as P

ADAPTER_SCALE = 2.0
ROPE_BASE = 500000.0
MESH = pl.DeviceIdType.MESH
BF16 = jnp.bfloat16
F32 = jnp.float32
NT = (((1,), (1,)), ((), ()))
NEGATIVE = -1e30
SENDS = 176
LOCALS = 64


def mm(a, b):
    return jnp.dot(a, b, preferred_element_type=F32)


def kernel(
    hidden, lists, slots, lengths, frequencies,
    query_w, kv_w, out_w, down, up_q, up_kv, down_o, up_o, keys, values,
    out,
    z_all, h_a, h_b, d_a, d_b, u_a, u_b, p_all, o_a, o_b, w_all, w_out, k_all, v_all,
    acc, low_send_a, low_recv_a, low_send_b, low_recv_b, low_parts, out_parts,
    low_mine, low_theirs,
    q_rows, key_rows, value_rows, length_rows, mixed_rows,
    sib_send, sib_recv, own_sum, lists_v, slots_v, lengths_v, frequencies_v, id_columns_a, id_columns_b,
    low_a, low_b, out_low_a, out_low_b, *sums,
):
    (
        z_far, z_half, z_near, z_back, x_far, x_half, x_near, x_back, y_far, y_half, y_near, y_back,
        xu_far, xu_half, xu_near, xu_back, yu_far, yu_half, yu_near, yu_back,
        send_sem, recv_sem, local_sem,
    ) = sums
    replica = lax.axis_index("replica")
    t = lax.axis_index("tensor")
    x, y = replica // 4, replica % 4
    z, c = t // 2, t % 2
    other = 1 - c

    def wrap(v):
        return lax.rem(v + 4, 4)

    def at_x(d):
        return (wrap(x + d) * 4 + y, t)

    def at_y(d):
        return (x * 4 + wrap(y + d), t)

    def at_z(d):
        return (replica, wrap(z + d) * 2 + c)

    sibling = (replica, z * 2 + other)

    counts = {"send": 0, "local": 0}
    sent = []

    def send(src, dst, device):
        i = counts["send"]
        counts["send"] = i + 1
        copy = pltpu.make_async_remote_copy(
            src_ref=src, dst_ref=dst, send_sem=send_sem.at[i], recv_sem=recv_sem.at[i],
            device_id=device, device_id_type=MESH,
        )
        copy.start()
        sent.append(copy)
        return copy

    def local(src, dst):
        i = counts["local"]
        counts["local"] = i + 1
        copy = pltpu.make_async_copy(src, dst, local_sem.at[i])
        copy.start()
        return copy

    barrier = pltpu.get_barrier_semaphore()
    partners = [at_x(d) for d in (1, 2, 3)] + [at_y(d) for d in (1, 2, 3)]
    partners += [(replica, lax.rem(t + i, 8)) for i in range(1, 8)]
    for partner in partners:
        pl.semaphore_signal(barrier, inc=1, device_id=partner, device_id_type=MESH)

    own_small = [local(lists, lists_v), local(slots, slots_v)]
    own_h = [
        local(hidden.at[:, 0:512], h_a.at[x, 0:128]),
        local(hidden.at[:, 512:1024], h_b.at[y, 0:128]),
        local(hidden, z_all.at[t]),
    ]
    own_d = [
        local(down.at[:, :, 0:512], d_a.at[y]),
        local(down.at[:, :, 512:1024], d_b.at[x]),
    ]
    own_u = [
        local(up_q.at[:, :, 0:256], u_a.at[y, :, :, 0:256]),
        local(up_kv.at[:, 0], u_a.at[y, :, :, 256:384]),
        local(up_q.at[:, :, 256:512], u_b.at[x, :, :, 0:256]),
        local(up_kv.at[:, 1], u_b.at[x, :, :, 256:384]),
    ]
    own_p = local(down_o, p_all.at[x, y])
    own_o = [
        local(up_o.at[:, :, 0:512], o_a.at[y]),
        local(up_o.at[:, :, 512:1024], o_b.at[x]),
    ]
    own_late = [local(lengths, lengths_v), local(frequencies, frequencies_v)]

    for copy in own_small:
        copy.wait()
    wanted = lists_v[pl.ds(replica, 1), :].astype(F32).astype(BF16)
    picked = lax.broadcasted_iota(jnp.int32, (32, 128), 0) == slots_v[...]
    own_ids = mm(jnp.broadcast_to(wanted, (16, 32)), picked.astype(F32).astype(BF16))
    id_rows = jnp.concatenate([own_ids] * 4, axis=1).astype(BF16)
    for copy in own_h:
        copy.wait()
    h_a[x, 128:144, :] = id_rows
    h_b[y, 128:144, :] = id_rows
    pl.semaphore_wait(barrier, len(partners))

    arrived = set()

    def landed(copies):
        for copy in copies:
            if id(copy) not in arrived:
                arrived.add(id(copy))
                copy.wait_recv()

    def ring_rest(lo, hi, own, device):
        return [
            send(hi(own), hi(own), device(1)),
            send(lo(own), lo(own), device(-1)),
        ]

    def ring_one(lo, hi, own, device):
        return [
            send(lo(own), lo(own), device(1)),
            send(hi(own), hi(own), device(-1)),
        ] + ring_rest(lo, hi, own, device)

    def ring_two(first, lo, hi, own, device):
        before, after = wrap(own - 1), wrap(own + 1)
        landed(first[0:1])
        onward = [send(lo(before), lo(before), device(1))]
        landed(first[1:2])
        onward.append(send(hi(after), hi(after), device(-1)))
        return first + onward

    def pool_parts(pool):
        return (
            (lambda i: pool.at[i, y, 0:2], lambda i: pool.at[i, y, 2:4], x, at_x),
            (lambda i: pool.at[x, i, 4:6], lambda i: pool.at[x, i, 6:8], y, at_y),
            (lambda i: pool.at[:, i, 0:2], lambda i: pool.at[:, i, 2:4], y, at_y),
            (lambda i: pool.at[i, :, 4:6], lambda i: pool.at[i, :, 6:8], x, at_x),
        )

    def gather_one(pool):
        parts = pool_parts(pool)
        return ring_one(*parts[0]), ring_one(*parts[1])

    def gather_two(pool, a, b):
        parts = pool_parts(pool)
        return ring_two(a, *parts[0]), ring_two(b, *parts[1])

    def gather_four(pool, a, b):
        parts = pool_parts(pool)
        return ring_two(a, *parts[2]), ring_two(b, *parts[3])

    ha_parts = (lambda i: h_a.at[i, 0:80], lambda i: h_a.at[i, 80:144], x, at_x)
    hb_parts = (lambda i: h_b.at[i, 0:80], lambda i: h_b.at[i, 80:144], y, at_y)
    z_parts = (lambda i: z_all.at[i * 2 + c, 0:64], lambda i: z_all.at[i * 2 + c, 64:128], z, at_z)
    da_parts = (lambda i: d_a.at[i, 0:4], lambda i: d_a.at[i, 4:8], y, at_y)
    db_parts = (lambda i: d_b.at[i, 0:4], lambda i: d_b.at[i, 4:8], x, at_x)
    ua_parts = (lambda i: u_a.at[i, 0:4], lambda i: u_a.at[i, 4:8], y, at_y)
    ub_parts = (lambda i: u_b.at[i, 0:4], lambda i: u_b.at[i, 4:8], x, at_x)
    oa_parts = (lambda i: o_a.at[i, 0:4], lambda i: o_a.at[i, 4:8], y, at_y)
    ob_parts = (lambda i: o_b.at[i, 0:4], lambda i: o_b.at[i, 4:8], x, at_x)

    ha1 = ring_one(*ha_parts)
    hb1 = ring_one(*hb_parts)
    z1 = ring_one(*z_parts)
    s0 = send(z_all.at[t], z_all.at[t], sibling)
    for copy in own_d:
        copy.wait()
    da1 = ring_one(*da_parts)
    db1 = ring_one(*db_parts)

    w_copies = []
    for d in range(8):
        i = lax.rem(t + d, 8)
        w_copies.append(local(query_w.at[i], w_all.at[i, :, 0:512]))
        w_copies.append(local(kv_w.at[0, i], w_all.at[i, :, 512:640]))
        w_copies.append(local(kv_w.at[1, i], w_all.at[i, :, 640:768]))
    k_copy = local(keys, k_all)
    v_copy = local(values, v_all)
    o_copies = []
    for d in (2, 1, 3, 0):
        for core in (other, c):
            i = wrap(z + d) * 2 + core
            columns = pl.ds(pl.multiple_of(i * 1024, 1024), 1024)
            o_copies.append(local(out_w.at[:, columns], w_out.at[i]))

    ha2 = ring_two(ha1, *ha_parts)
    hb2 = ring_two(hb1, *hb_parts)
    z2 = ring_two(z1, *z_parts)
    landed(z1)
    up_z, down_z = wrap(z + 1), wrap(z - 1)
    s1 = send(z_all.at[up_z * 2 + c], z_all.at[up_z * 2 + c], sibling)
    s2 = send(z_all.at[down_z * 2 + c], z_all.at[down_z * 2 + c], sibling)
    da2 = ring_two(da1, *da_parts)
    db2 = ring_two(db1, *db_parts)

    for copy in w_copies:
        copy.wait()
    acc[...] = jnp.zeros_like(acc)

    def project(i):
        acc[...] += mm(z_all[i], w_all[i])

    def project_near(i, _):
        project(wrap(z + i + i // 2) * 2 + c)
        return 0

    lax.fori_loop(0, 3, project_near, 0)

    for copy in own_late:
        copy.wait()

    def column(row):
        return jnp.transpose(jnp.broadcast_to(row, (128, 128)), (1, 0))

    row_lengths = column(lengths_v[...].astype(F32))
    angles = row_lengths * frequencies_v[...]
    lane = lax.broadcasted_iota(jnp.int32, (128, 128), 1)
    cosines = jnp.cos(angles)
    sines = jnp.where(lane < 64, -jnp.sin(angles), jnp.sin(angles))
    for i in range(8):
        length_rows[pl.ds(i, 128, stride=8), :] = row_lengths


    landed(z2)
    far = wrap(z + 2) * 2 + c
    s3 = send(z_all.at[far], z_all.at[far], sibling)
    landed((s0, s1, s2))

    def project_far(i, _):
        mine = wrap(z + 2) * 2 + c
        theirs = wrap(z + i + i // 2) * 2 + other
        project(jnp.where(i == 3, mine, theirs))
        return 0

    lax.fori_loop(0, 4, project_far, 0)
    landed((s3,))
    project(wrap(z + 2) * 2 + other)

    landed(ha2)
    landed(hb2)

    def ids_of(h):
        return jnp.concatenate(
            [h[i, 128:144, 0:128].astype(F32)[0:1] for i in range(4)], axis=1
        )

    def fold(h, d, ids, j, owner, total):
        rows = h[:, 0:128, :].reshape(512, 512)
        maps = d[j].reshape(384, 512)
        every = lax.dot_general(maps, rows, NT, preferred_element_type=F32)
        every = every.reshape(8, 48, 512)
        first = (owner * 8).astype(F32)
        for i in range(8):
            total = total + jnp.where(ids == first + float(i), every[i], 0.0)
        return total

    ids_a, ids_b = ids_of(h_a), ids_of(h_b)
    for i in range(4):
        id_columns_a[i] = column(ids_a[:, i * 128 : (i + 1) * 128])
        id_columns_b[i] = column(ids_b[:, i * 128 : (i + 1) * 128])
    landed(da1)
    landed(db1)
    zero_low = jnp.zeros((48, 512), F32)

    def near_a(i, total):
        j = wrap(y + i + i // 2)
        return fold(h_a, d_a, ids_a, j, x * 4 + j, total)

    def near_b(i, total):
        j = wrap(x + i + i // 2)
        return fold(h_b, d_b, ids_b, j, j * 4 + y, total)

    sum_a = lax.fori_loop(0, 3, near_a, zero_low)
    sum_b = lax.fori_loop(0, 3, near_b, zero_low)
    landed(da2)
    sum_a = fold(h_a, d_a, ids_a, wrap(y + 2), x * 4 + wrap(y + 2), sum_a)
    for i in range(4):
        low_send_a[i] = sum_a[:, i * 128 : (i + 1) * 128]
    back_a = [
        send(low_send_a.at[wrap(x + d)], low_recv_a.at[x], at_x(d)) for d in (1, 3, 2)
    ]
    landed(db2)
    sum_b = fold(h_b, d_b, ids_b, wrap(x + 2), wrap(x + 2) * 4 + y, sum_b)
    for i in range(4):
        low_send_b[i] = sum_b[:, i * 128 : (i + 1) * 128]
    back_b = [
        send(low_send_b.at[wrap(y + d)], low_recv_b.at[y], at_y(d)) for d in (1, 3, 2)
    ]

    own_p.wait()
    pa1, pb1 = gather_one(p_all)
    for copy in own_u:
        copy.wait()
    ua1 = ring_one(*ua_parts)
    ub1 = ring_one(*ub_parts)
    landed(back_a)
    landed(back_b)
    part = low_send_a[x] + low_send_b[y]
    for d in (1, 2, 3):
        part = part + low_recv_a[wrap(x + d)] + low_recv_b[wrap(y + d)]
    def over_tensor(part, mine, theirs, parts, forward_first, forward):
        mine[...] = part
        to_core = send(mine, theirs, sibling)
        forward_first()
        landed([to_core])
        parts[z] = part + theirs[...]
        copies = [send(parts.at[z], parts.at[z], at_z(d)) for d in (2, 1, 3)]
        forward()
        landed(copies)
        return (parts[0] + parts[1]) + (parts[2] + parts[3])

    def piece(lo, hi, first, second):
        return (
            [
                send(p_all.at[lo:hi, y, first : first + 2], p_all.at[lo:hi, y, first : first + 2], at_y(1)),
                send(p_all.at[lo:hi, y, second : second + 2], p_all.at[lo:hi, y, second : second + 2], at_y(-1)),
            ],
            [
                send(p_all.at[x, lo:hi, first + 4 : first + 6], p_all.at[x, lo:hi, first + 4 : first + 6], at_x(1)),
                send(p_all.at[x, lo:hi, second + 4 : second + 6], p_all.at[x, lo:hi, second + 4 : second + 6], at_x(-1)),
            ],
        )

    pools = []

    def forward_p():
        pools.extend(gather_two(p_all, pa1, pb1))

    def forward_u():
        pools.append(ring_two(ua1, *ua_parts))
        pools.append(ring_two(ub1, *ub_parts))
        landed(pools[0] + pools[1])
        pools.extend(piece(0, 2, 0, 2))

    low = over_tensor(part, low_mine, low_theirs, low_parts, forward_p, forward_u)
    pa2, pb2, ua2, ub2, pa3, pb3 = pools

    def spread(low, first):
        source = lax.broadcasted_iota(jnp.int32, (128, 128), 0)
        target = lax.broadcasted_iota(jnp.int32, (128, 128), 1)
        pattern = (source == first + lax.rem(target, 16)).astype(F32).astype(BF16)
        return mm(low, pattern)

    lane_adapter = (lane // 16).astype(F32)

    def turned(low):
        padding = jnp.zeros((128 - low.shape[0], 128), F32)
        full = jnp.concatenate([low.astype(F32), padding], axis=0)
        return jnp.transpose(full, (1, 0)).astype(BF16)

    class RingSum:
        def __init__(self, far, half, near, back, device):
            self.far_block, self.half, self.near_block, self.back = far, half, near, back
            self.device = device

        def far(self, block):
            self.far_block[...] = block.astype(BF16)
            self.halves = [
                send(self.far_block.at[0:64], self.half.at[0], self.device(1)),
                send(self.far_block.at[64:128], self.half.at[1], self.device(-1)),
            ]

        def near(self, plus, minus):
            near, back = self.near_block, self.back
            self.waiting = plus[0:64], minus[64:128]
            near[0, 64:128] = plus[64:128].astype(BF16)
            near[1, 0:64] = minus[0:64].astype(BF16)
            self.blocks = [
                send(near.at[0, 64:128], back.at[0, 64:128], self.device(1)),
                send(near.at[1, 0:64], back.at[1, 0:64], self.device(-1)),
            ]

        def join(self):
            near, back = self.near_block, self.back
            landed(self.halves[0:1])
            near[0, 0:64] = (self.waiting[0] + self.half[0].astype(F32)).astype(BF16)
            self.blocks.append(send(near.at[0, 0:64], back.at[0, 0:64], self.device(1)))
            landed(self.halves[1:2])
            near[1, 64:128] = (self.waiting[1] + self.half[1].astype(F32)).astype(BF16)
            self.blocks.append(send(near.at[1, 64:128], back.at[1, 64:128], self.device(-1)))

        def total(self):
            landed(self.blocks)
            return self.back[0].astype(F32) + self.back[1].astype(F32)

    def expand(g, columns, rows, owner):
        blocks = []
        for j in range(4):
            first = (owner(j) * 8).astype(F32)
            blocks.append(jnp.where(columns[g] == lane_adapter + first, rows, 0.0).astype(BF16))
        return jnp.concatenate(blocks, axis=1)

    def owner_a(j):
        return x * 4 + j

    def owner_b(j):
        return j * 4 + y

    low_a[x] = low.astype(BF16)
    low_b[y] = low.astype(BF16)
    around_a = [send(low_a.at[x], low_a.at[x], at_x(d)) for d in (2, 1, 3)]
    around_b = [send(low_b.at[y], low_b.at[y], at_y(d)) for d in (2, 1, 3)]
    more_a, more_b = piece(2, 4, 0, 2)
    pa3, pb3 = pa3 + more_a, pb3 + more_b
    landed(ua2)
    landed(ub2)

    def raised(g, columns, lows, first, owner, maps):
        rows = turned(lows[g])
        for_q = expand(g, columns, spread(rows, 0), owner)
        for_kv = expand(g, columns, spread(rows, first), owner)
        return ADAPTER_SCALE * jnp.concatenate(
            [
                mm(for_q, maps[:, :, :, 0:256].reshape(512, 256)),
                mm(for_kv, maps[:, :, :, 256:384].reshape(512, 128)),
            ],
            axis=1,
        )

    def raised_a(d):
        return raised(wrap(x + d), id_columns_a, low_a, 16, owner_a, u_a)

    def raised_b(d):
        return raised(wrap(y + d), id_columns_b, low_b, 32, owner_b, u_b)

    xu = RingSum(xu_far, xu_half, xu_near, xu_back, at_x)
    yu = RingSum(yu_far, yu_half, yu_near, yu_back, at_y)
    landed(around_a[0:1])
    xu.far(raised_a(2))
    landed(around_b[0:1])
    yu.far(raised_b(2))
    rest_a, rest_b = piece(0, 2, 2, 0)
    landed(around_a)
    xu.near(raised_a(1), raised_a(3))
    landed(around_b)
    yu.near(raised_b(1), raised_b(3))
    own_a, own_b = raised_a(0), raised_b(0)
    xu.join()
    yu.join()
    landed(pa3 + pb3)
    pa4, pb4 = gather_four(p_all, pa3, pb3)
    more_a, more_b = piece(2, 4, 2, 0)
    pa4, pb4 = pa4 + rest_a + more_a, pb4 + rest_b + more_b
    for copy in own_o:
        copy.wait()
    oa1 = ring_one(*oa_parts)
    ob1 = ring_one(*ob_parts)
    own_a = own_a + xu.total()
    acc[:, 0:256] += own_a[:, 0:256]
    acc[:, 512:640] += own_a[:, 256:384]
    own_b = own_b + yu.total()
    acc[:, 256:512] += own_b[:, 0:256]
    acc[:, 640:768] += own_b[:, 256:384]

    def rotated(columns):
        flat = acc[:, columns * 128 : (columns + 1) * 128]
        moved = flat * cosines + pltpu.roll(flat, 64, 1) * sines
        return moved.astype(BF16).astype(F32)

    new_key = rotated(4)
    new_value = acc[:, 640:768].astype(BF16).astype(F32)
    for i in range(8):
        rows = pl.ds(i, 128, stride=8)
        q_rows[rows, :] = rotated(i % 4)
        key_rows[rows, :] = new_key
        value_rows[rows, :] = new_value

    k_copy.wait()
    v_copy.wait()
    scale = 1.0 / (128.0 ** 0.5)

    def attend(b, _):
        first = pl.multiple_of(b * 256, 256)
        rows = pl.ds(first, 256)
        q = q_rows[rows, :]
        q16 = q.astype(BF16)
        scores = []
        for i in range(16):
            pair = k_all[pl.ds(b * 32 + 2 * i, 2)].reshape(256, 128)
            both = lax.dot_general(
                q16[i * 16 : (i + 1) * 16], pair, NT, preferred_element_type=F32
            )
            scores.append(both[0:8, 0:128])
            scores.append(both[8:16, 128:256])
        scores = jnp.concatenate(scores, axis=0) * scale
        self_score = jnp.sum(q * key_rows[rows, :], axis=1, keepdims=True) * scale
        slot = lax.broadcasted_iota(jnp.int32, (256, 128), 1).astype(F32)
        valid = slot < length_rows[rows, :]
        highest = jnp.maximum(
            jnp.max(jnp.where(valid, scores, NEGATIVE), axis=1, keepdims=True), self_score
        )
        weights = jnp.where(valid, jnp.exp(scores - highest), 0.0)
        self_weight = jnp.exp(self_score - highest)
        total = jnp.sum(weights, axis=1, keepdims=True) + self_weight
        weights = weights / total
        even = lax.rem(lax.broadcasted_iota(jnp.int32, (256, 128), 0), 16) < 8
        weights16 = jnp.concatenate(
            [jnp.where(even, weights, 0.0), jnp.where(even, 0.0, weights)], axis=1
        ).astype(BF16)
        self16 = (self_weight / total).astype(BF16).astype(F32)
        mixed = []
        for i in range(16):
            pair = v_all[pl.ds(b * 32 + 2 * i, 2)].reshape(256, 128)
            mixed.append(mm(weights16[i * 16 : (i + 1) * 16], pair))
        mixed_rows[rows, :] = jnp.concatenate(mixed, axis=0) + self16 * value_rows[rows, :]
        return 0

    lax.fori_loop(0, 4, attend, 0)
    attended = jnp.concatenate(
        [mixed_rows[pl.ds(i, 128, stride=8), :].astype(BF16) for i in range(4)], axis=1
    )

    before_output = len(sent)

    for copy in o_copies:
        copy.wait()
    to_sibling = {}
    for d in (2, 1, 3, 0):
        i = wrap(z + d)
        sib_send[i] = mm(attended, w_out[i * 2 + other]).astype(BF16)
        to_sibling[d] = send(sib_send.at[i], sib_recv.at[i], sibling)

    landed(pa4 + pb4)
    own_row = own_ids[0:1]
    low_out = jnp.zeros((16, 128), F32)
    for j in range(4):
        maps = p_all[j].reshape(512, 512)
        every = lax.dot_general(maps, attended, NT, preferred_element_type=F32)
        every = every.reshape(32, 16, 128)
        for i in range(32):
            low_out = low_out + jnp.where(own_row == float(j * 32 + i), every[i], 0.0)
    out_parts[t] = low_out
    out_over_t = [
        send(out_parts.at[t], out_parts.at[t], (replica, lax.rem(t + i, 8))) for i in range(1, 8)
    ]

    def chip_sum(d):
        i = wrap(z + d)
        mine = mm(attended, w_out[i * 2 + c])
        landed([to_sibling[d]])
        return mine + sib_recv[i].astype(F32)

    oa2 = ring_two(oa1, *oa_parts)
    ob2 = ring_two(ob1, *ob_parts)
    over_z = RingSum(z_far, z_half, z_near, z_back, at_z)
    over_z.far(chip_sum(2))
    over_z.near(chip_sum(1), chip_sum(3))

    landed(out_over_t)
    low_out = out_parts[0]
    for i in range(1, 8):
        low_out = low_out + out_parts[i]
    out_low_a[x] = low_out.astype(BF16)
    out_low_b[y] = low_out.astype(BF16)
    around_a = [send(out_low_a.at[x], out_low_a.at[x], at_x(d)) for d in (2, 1, 3)]
    around_b = [send(out_low_b.at[y], out_low_b.at[y], at_y(d)) for d in (2, 1, 3)]
    for copy in sent[:before_output]:
        copy.wait_send()
    over_z.join()

    def product(g, columns, lows, owner, maps):
        expanded = expand(g, columns, spread(turned(lows[g]), 0), owner)
        return ADAPTER_SCALE * mm(expanded, maps[...].reshape(512, 512))

    def product_a(d):
        return product(wrap(x + d), id_columns_a, out_low_a, owner_a, o_a)

    def product_b(d):
        return product(wrap(y + d), id_columns_b, out_low_b, owner_b, o_b)

    landed(oa2)
    landed(ob2)
    over_x = RingSum(x_far, x_half, x_near, x_back, at_x)
    over_y = RingSum(y_far, y_half, y_near, y_back, at_y)
    landed(around_a[0:1])
    over_x.far(product_a(2))
    landed(around_b[0:1])
    over_y.far(product_b(2))
    landed(around_a)
    over_x.near(product_a(1), product_a(3))
    landed(around_b)
    over_y.near(product_b(1), product_b(3))
    over_x.join()
    over_y.join()
    own_sum[...] = chip_sum(0)
    own_sum[:, 0:512] += product_a(0)
    own_sum[:, 512:1024] += product_b(0)
    own_sum[...] += over_z.total()
    out[:, 0:512] = own_sum[:, 0:512] + over_x.total()
    out[:, 512:1024] = own_sum[:, 512:1024] + over_y.total()

    for copy in sent[before_output:]:
        copy.wait_send()


def shards(
    hidden,
    query_weight,
    keyvalue_weight,
    output_weight,
    adapter_down_maps,
    adapter_up_query,
    adapter_up_keyvalue,
    adapter_down_output,
    adapter_up_output,
    cached_keys,
    cached_values,
    context_lengths,
    request_list_slots,
    group_adapter_lists,
):
    pairs = np.arange(64, dtype=np.float32) * np.float32(2.0) / np.float32(128.0)
    frequency = np.power(np.float32(ROPE_BASE), -pairs).astype(np.float32)
    frequencies = jnp.asarray(np.concatenate([frequency, frequency])[None, :])

    hbm = pl.BlockSpec(memory_space=pl.ANY)
    vmem = pl.BlockSpec(memory_space=pltpu.VMEM)
    result = pl.pallas_call(
        kernel,
        out_shape=jax.ShapeDtypeStruct((128, 1024), F32),
        in_specs=[hbm] * 15,
        out_specs=vmem,
        scratch_shapes=[
            pltpu.VMEM((8, 128, 1024), BF16),
            pltpu.VMEM((4, 144, 512), BF16),
            pltpu.VMEM((4, 144, 512), BF16),
            pltpu.VMEM((4, 8, 48, 512), BF16),
            pltpu.VMEM((4, 8, 48, 512), BF16),
            pltpu.VMEM((4, 8, 16, 384), BF16),
            pltpu.VMEM((4, 8, 16, 384), BF16),
            pltpu.VMEM((4, 4, 8, 16, 512), BF16),
            pltpu.VMEM((4, 8, 16, 512), BF16),
            pltpu.VMEM((4, 8, 16, 512), BF16),
            pltpu.VMEM((8, 1024, 768), BF16),
            pltpu.VMEM((8, 512, 1024), BF16),
            pltpu.VMEM((128, 128, 128), BF16),
            pltpu.VMEM((128, 128, 128), BF16),
            pltpu.VMEM((128, 768), F32),
            pltpu.VMEM((4, 48, 128), F32),
            pltpu.VMEM((4, 48, 128), F32),
            pltpu.VMEM((4, 48, 128), F32),
            pltpu.VMEM((4, 48, 128), F32),
            pltpu.VMEM((4, 48, 128), F32),
            pltpu.VMEM((8, 16, 128), F32),
            pltpu.VMEM((48, 128), F32),
            pltpu.VMEM((48, 128), F32),
            pltpu.VMEM((1024, 128), F32),
            pltpu.VMEM((1024, 128), F32),
            pltpu.VMEM((1024, 128), F32),
            pltpu.VMEM((1024, 128), F32),
            pltpu.VMEM((1024, 128), F32),
            pltpu.VMEM((4, 128, 1024), BF16),
            pltpu.VMEM((4, 128, 1024), BF16),
            pltpu.VMEM((128, 1024), F32),
            pltpu.VMEM((16, 32), jnp.int32),
            pltpu.VMEM((1, 128), jnp.int32),
            pltpu.VMEM((1, 128), jnp.int32),
            pltpu.VMEM((1, 128), F32),
            pltpu.VMEM((4, 128, 128), F32),
            pltpu.VMEM((4, 128, 128), F32),
            pltpu.VMEM((4, 48, 128), BF16),
            pltpu.VMEM((4, 48, 128), BF16),
            pltpu.VMEM((4, 16, 128), BF16),
            pltpu.VMEM((4, 16, 128), BF16),
            pltpu.VMEM((128, 1024), BF16),
            pltpu.VMEM((2, 64, 1024), BF16),
            pltpu.VMEM((2, 128, 1024), BF16),
            pltpu.VMEM((2, 128, 1024), BF16),
            pltpu.VMEM((128, 512), BF16),
            pltpu.VMEM((2, 64, 512), BF16),
            pltpu.VMEM((2, 128, 512), BF16),
            pltpu.VMEM((2, 128, 512), BF16),
            pltpu.VMEM((128, 512), BF16),
            pltpu.VMEM((2, 64, 512), BF16),
            pltpu.VMEM((2, 128, 512), BF16),
            pltpu.VMEM((2, 128, 512), BF16),
            pltpu.VMEM((128, 384), BF16),
            pltpu.VMEM((2, 64, 384), BF16),
            pltpu.VMEM((2, 128, 384), BF16),
            pltpu.VMEM((2, 128, 384), BF16),
            pltpu.VMEM((128, 384), BF16),
            pltpu.VMEM((2, 64, 384), BF16),
            pltpu.VMEM((2, 128, 384), BF16),
            pltpu.VMEM((2, 128, 384), BF16),
            pltpu.SemaphoreType.DMA((SENDS,)),
            pltpu.SemaphoreType.DMA((SENDS,)),
            pltpu.SemaphoreType.DMA((LOCALS,)),
        ],
        compiler_params=pltpu.CompilerParams(
            collective_id=0, has_side_effects=True, vmem_limit_bytes=62 * 1024 * 1024
        ),
        cost_estimate=pl.CostEstimate(flops=8_000_000_000, bytes_accessed=32_000_000, transcendentals=0),
    )(
        hidden,
        group_adapter_lists,
        request_list_slots[None, :],
        context_lengths[None, :],
        frequencies,
        query_weight.reshape(8, 1024, 512),
        keyvalue_weight.reshape(2, 8, 1024, 128),
        output_weight,
        jnp.transpose(adapter_down_maps, (0, 2, 1)),
        adapter_up_query,
        adapter_up_keyvalue,
        jnp.transpose(adapter_down_output, (0, 2, 1)),
        adapter_up_output,
        cached_keys.reshape(128, 128, 128),
        cached_values.reshape(128, 128, 128),
    )
    return result.astype(BF16)


def solution(mesh):
    in_specs = (
        P("replica", "tensor"),
        P(None, "tensor"),
        P(None, None, "tensor"),
        P("tensor", None),
        P("replica", "tensor", None),
        P("replica", None, "tensor"),
        P("replica", None, None, "tensor"),
        P("replica", "tensor", None),
        P("replica", None, "tensor"),
        P("replica", "tensor", None, None),
        P("replica", "tensor", None, None),
        P("replica"),
        P("replica"),
        P(),
    )
    out_specs = P("replica", "tensor")
    return jax.shard_map(shards, mesh=mesh, in_specs=in_specs, out_specs=out_specs, check_vma=False)
```
